256 devices in a mesh: grp: 8 (over y, core), cls: 32 (over x, z).
Axes of the slice: x: 4, y: 4, z: 8, core: 2. Of those that a mesh axis runs over, the one named last changes fastest.
Arguments:
- particles: float32 [8192, 128, 128], P(('grp', 'cls')), may hold values from -6 to 6
- references: float32 [1024, 2, 128, 128], P('cls'), may hold values from -6 to 6
- class_of: int32 [8192], P(('grp', 'cls')), may hold values from 0 to 1023, as said below
- rotation_bin: int32 [8192], P(('grp', 'cls')), may hold values from 0 to 3
- shift_best: int32 [8192], P(('grp', 'cls')), may hold values from 0 to 63
- defocus_bin: int32 [8192], P(('grp', 'cls')), may hold values from 0 to 15
- shift_list: int32 [64, 2], replicated, may hold values from -8 to 8
- defocus: float32 [16], replicated, may hold values from 8 to 64
Outputs:
- scores: float32 [8192, 64], P(('grp', 'cls'))
- new_references: float32 [1024, 2, 128, 128], P(('cls', 'grp'))
The draws below stay inside these ranges and needn't reach their ends.
Inputs may be any that keep to these rules, and one draw needn't show every extreme that they name: `class_of`: class c belongs to owner c // 32. Among the 32 particles of one device (aligned blocks of 32 rows), at most 2 belong to the classes of one owner, and in every draw one owner holds exactly 2 from every device.
All inputs are finite; a program needn't handle non-finite values.
Results may differ from the reference program's by a relative error of at most 0.0003.
Values sent between devices are 32-bit elements; how exact they have to be, the bound alone decides.
No kernel may reach another device: no remote copies, remote signals or barrier semaphores. Data moves between devices by JAX's collectives and lax.ppermute only.
A program may use at most 128 MiB of HBM per device.

```python
import math
import jax
import jax.numpy as jnp
from jax import lax

IMG = 128
NSHIFT = 64
NDEF = 16
CLS_DEV = 32
PART_DEV = 32
CLASSES = 1024
PARTICLES = 8192
CAP = 2
N_GRP = 8
N_CLS = 32


def draw_class_of(key, part):
    key = jax.random.fold_in(key, 7)
    key_level, key_heavy, key_noise, key_order, key_local = jax.random.split(key, 5)
    slot_total = N_CLS * CAP
    blocks = N_GRP * N_CLS
    slot_owner = jnp.arange(slot_total, dtype=jnp.int32) // CAP
    busy_level = jax.random.randint(key_level, (N_CLS,), 0, 4)
    heavy_owner = jax.random.randint(key_heavy, (), 0, N_CLS)
    noise_draw = jax.random.randint(key_noise, (blocks, slot_total), 0, 4096)
    priority = noise_draw + busy_level[slot_owner] * 2048 + jnp.where(slot_owner == heavy_owner, 65536, 0)
    priority = priority * slot_total + jnp.arange(slot_total, dtype=jnp.int32)
    picked = lax.top_k(priority, PART_DEV)[1]
    owners = slot_owner[picked]
    shuffle_keys = jax.random.randint(key_order, (blocks, PART_DEV), 0, 65536) * PART_DEV + jnp.arange(PART_DEV, dtype=jnp.int32)
    shuffle_order = jnp.argsort(shuffle_keys, axis=1, stable=True)
    owners = jnp.take_along_axis(owners, shuffle_order, axis=1)
    local_class = jax.random.randint(key_local, (blocks, PART_DEV), 0, CLS_DEV)
    return (owners * CLS_DEV + local_class).reshape(blocks * PART_DEV).astype(jnp.int32)


def plant(result, stream_key, least, largest):
    extent = result.shape
    index_at = [jax.random.randint(jax.random.fold_in(stream_key, axis), (), 0, extent[axis]) for axis in range(len(extent))]
    result = result.at[tuple(index_at)].set(least)
    longest = extent.index(max(extent))
    index_at[longest] = (index_at[longest] + 1) % extent[longest]
    return result.at[tuple(index_at)].set(largest)


def steps_of(stream_key, shape, cuts, smallest, top_value):
    gain = 1.0
    for axis_at, blocks in cuts:
        draws = jax.random.uniform(jax.random.fold_in(jax.random.fold_in(stream_key, 6), axis_at), (blocks,), jnp.float32, smallest / len(cuts), top_value / len(cuts))
        gain = gain * jnp.repeat(jnp.exp(draws), shape[axis_at] // blocks).reshape((-1,) + (1,) * (len(shape) - 1 - axis_at))
    return gain


def normal_values(rng, dims, scale, most, cuts=(), kind=jnp.bfloat16):
    gain = steps_of(rng, dims, cuts, -0.22, 0.18) if cuts else 1.0
    drawn = jax.random.normal(rng, dims, jnp.float32) * scale * gain
    return jnp.minimum(jnp.maximum(drawn, -most), most).astype(kind)


def setup_inputs(seed: int = 0) -> dict:
    arg_keys = jax.random.split(jax.random.key(seed), 9)
    return {
        "particles": normal_values(arg_keys[0], (PARTICLES, IMG, IMG), 1.0, 6.0, ((0, 256),), jnp.float32),
        "references": normal_values(arg_keys[1], (CLASSES, 2, IMG, IMG), 1.0, 6.0, ((0, 32),), jnp.float32),
        "class_of": draw_class_of(jax.random.fold_in(arg_keys[8], 71), 0),
        "rotation_bin": plant(jax.random.randint(arg_keys[3], (PARTICLES,), 0, 4), jax.random.fold_in(arg_keys[3], 1), 0, 3).astype(jnp.int32),
        "shift_best": plant(jax.random.randint(arg_keys[4], (PARTICLES,), 0, NSHIFT), jax.random.fold_in(arg_keys[4], 1), 0, NSHIFT - 1).astype(jnp.int32),
        "defocus_bin": plant(jax.random.randint(arg_keys[5], (PARTICLES,), 0, NDEF), jax.random.fold_in(arg_keys[5], 1), 0, NDEF - 1).astype(jnp.int32),
        "shift_list": plant(jax.random.randint(arg_keys[6], (NSHIFT, 2), -8, 9), jax.random.fold_in(arg_keys[6], 1), -8, 8).astype(jnp.int32),
        "defocus": jnp.clip(jnp.exp(jax.random.uniform(arg_keys[7], (NDEF,), jnp.float32, math.log(8.0), math.log(64.0))), 8.0, 64.0),
    }


highest = lax.Precision.HIGHEST

def dft_tables(image_side):
    pixel_index = jnp.arange(image_side, dtype=jnp.int32)
    turn_grid = (pixel_index[:, None] * pixel_index[None, :] % image_side).astype(jnp.float32)
    angles = turn_grid * (2.0 * math.pi / image_side)
    norm_scale = 1.0 / math.sqrt(image_side)
    cos_table = jnp.cos(angles) * norm_scale
    sin_table = jnp.sin(angles) * norm_scale
    right_table = jnp.concatenate([cos_table, sin_table], axis=1)
    left_table = jnp.stack([jnp.stack([cos_table, -sin_table], axis=1), jnp.stack([-sin_table, -cos_table], axis=1)], axis=0)
    return (right_table, left_table)

def spectra(images, right_table, left_table):
    image_side = images.shape[-1]
    halfway = jnp.einsum('...jk,kl->...jl', images, right_table, precision=highest)
    halfway = halfway.reshape(halfway.shape[:-1] + (2, image_side))
    return jnp.einsum('aibj,...jbl->...ail', left_table, halfway, precision=highest)

def rotate(images, quarter_turns):
    turn_grid = quarter_turns[:, None, None]
    rot_one = jnp.rot90(images, 1, axes=(1, 2))
    rot_two = jnp.rot90(images, 2, axes=(1, 2))
    rot_three = jnp.rot90(images, 3, axes=(1, 2))
    return jnp.where(turn_grid == 0, images, jnp.where(turn_grid == 1, rot_one, jnp.where(turn_grid == 2, rot_two, rot_three)))

def contrast_table(defocus, image_side):
    pixel_index = jnp.arange(image_side, dtype=jnp.int32)
    signed = jnp.where(pixel_index < image_side // 2, pixel_index, pixel_index - image_side).astype(jnp.float32)
    radius = (signed[:, None] * signed[:, None] + signed[None, :] * signed[None, :]) / float((image_side // 2) ** 2)
    phases = defocus[:, None, None] * radius[None, :, :]
    return -(0.995 * jnp.sin(phases) + 0.1 * jnp.cos(phases))

def shift_tables(shift_list, image_side):
    pixel_index = jnp.arange(image_side, dtype=jnp.int32)
    turn_grid = (pixel_index[None, :, None] * shift_list[:, 0][:, None, None] + pixel_index[None, None, :] * shift_list[:, 1][:, None, None]) % image_side
    angles = turn_grid.astype(jnp.float32) * (2.0 * math.pi / image_side)
    return (jnp.cos(angles), jnp.sin(angles))

def make_score_table(shift_cos, shift_sin):
    shift_count = shift_cos.shape[0]
    return jnp.concatenate([shift_cos.reshape(shift_count, -1).T, -shift_sin.reshape(shift_count, -1).T], axis=0)

def particle_terms(spectrum, ref_rows, contrast, best_cos, best_sin, score_table, image_side):
    sign_pair = jnp.array([1.0, -1.0], jnp.float32)[None, :, None, None]
    swapped = spectrum[:, ::-1]
    ref_real = ref_rows[:, 0][:, None]
    ref_imag = ref_rows[:, 1][:, None]
    contrast_pair = contrast[:, None]
    product = contrast_pair * (spectrum * ref_real + swapped * ref_imag * sign_pair)
    item_count = spectrum.shape[0]
    scores = jnp.dot(product.reshape(item_count, -1), score_table, precision=highest, preferred_element_type=jnp.float32) / image_side
    contrib = contrast_pair * (spectrum * best_cos[:, None] - swapped * best_sin[:, None] * sign_pair)
    return (scores, contrib, contrast * contrast)

def reference(particles, references, class_of, rotation_bin, shift_best, defocus_bin, shift_list, defocus):
    image_side = particles.shape[-1]
    right_table, left_table = dft_tables(image_side)
    shift_cos, shift_sin = shift_tables(shift_list, image_side)
    score_table = make_score_table(shift_cos, shift_sin)
    block_rows = math.gcd(PARTICLES, 512)
    block_count = PARTICLES // block_rows

    def accumulate(running, block_start):
        numerator, weight_sum = running
        block_images = lax.dynamic_slice_in_dim(particles, block_start, block_rows, 0)
        block_class = lax.dynamic_slice_in_dim(class_of, block_start, block_rows, 0)
        block_turns = lax.dynamic_slice_in_dim(rotation_bin, block_start, block_rows, 0)
        block_best = lax.dynamic_slice_in_dim(shift_best, block_start, block_rows, 0)
        block_bins = lax.dynamic_slice_in_dim(defocus_bin, block_start, block_rows, 0)
        spectrum = spectra(rotate(block_images, block_turns), right_table, left_table)
        best_cos, best_sin = shift_tables(shift_list[block_best], image_side)
        contrast = contrast_table(defocus[block_bins], image_side)
        scores, contrib, weight = particle_terms(spectrum, references[block_class], contrast, best_cos, best_sin, score_table, image_side)
        numerator = numerator.at[block_class].add(contrib)
        weight_sum = weight_sum.at[block_class].add(weight)
        return ((numerator, weight_sum), scores)
    starts = jnp.arange(block_count, dtype=jnp.int32) * block_rows
    initial = (jnp.zeros((CLASSES, 2, image_side, image_side), jnp.float32), jnp.zeros((CLASSES, image_side, image_side), jnp.float32))
    (numerator, weight_sum), scores = lax.scan(accumulate, initial, starts)
    fresh_refs = numerator / (weight_sum[:, None] + 1.0)
    return (scores.reshape(PARTICLES, NSHIFT), fresh_refs)
```

```python
import functools
import math

import jax
import jax.numpy as jnp
import numpy as np
from jax import lax
from jax.experimental import pallas as pl
from jax.experimental.pallas import tpu as pltpu
from jax.sharding import PartitionSpec as P

HALF = 72
MIB = 1 << 20


def split_np(table):
    high = table.astype(jnp.bfloat16)
    low = (table - high.astype(np.float32)).astype(jnp.bfloat16)
    return high, low


def split(values):
    high = values.astype(jnp.bfloat16)
    low = (values - high.astype(jnp.float32)).astype(jnp.bfloat16)
    return high, low


def dft_constants(side):
    grid = np.outer(np.arange(side), np.arange(side)) % side
    angles = grid * (2.0 * np.pi / side)
    cos_table = (np.cos(angles) / np.sqrt(side)).astype(np.float32)
    sin_table = (np.sin(angles) / np.sqrt(side)).astype(np.float32)
    rows = side // 2 + 1
    left = np.zeros((2, HALF, side), np.float32)
    left[0, :rows] = cos_table[:rows]
    left[1, :rows] = sin_table[:rows]
    left_high, left_low = split_np(left.reshape(2 * HALF, side))
    left_table = np.concatenate(
        [
            np.concatenate([left_high, left_high], axis=1),
            np.concatenate([left_low, np.zeros_like(left_low)], axis=1),
        ],
        axis=0,
    )
    right = np.block([[cos_table, -sin_table], [-sin_table, -cos_table]]).astype(np.float32)
    right_high, right_low = split_np(right)
    return left_table, right_high, right_low


def turn_constants(side):
    row = np.arange(HALF)[:, None] + 0 * np.arange(side)[None, :]
    col = 0 * np.arange(HALF)[:, None] + np.arange(side)[None, :]
    shifts = np.stack([0 * row, row, row + col, col]) % side
    angles = shifts * (2.0 * np.pi / side)
    return np.concatenate([np.cos(angles), np.sin(angles)], axis=2).astype(np.float32)


def flip_constants(side):
    lanes = np.zeros((side, side), np.float32)
    lanes[(-np.arange(side)) % side, np.arange(side)] = 1.0
    fold = np.zeros((HALF, side), np.float32)
    for u in range(1, side // 2):
        fold[u, side - u] = 1.0
    unfold = np.zeros((side // 2, HALF), np.float32)
    for r in range(side // 2):
        unfold[r, side // 2 - r] = 1.0
    return lanes, fold, unfold


def scatter_kernel(class_local, class_ref, image_ref, slot_ref, count_ref, sems):
    for owner in range(count_ref.shape[0]):
        count_ref[owner] = 0
    copies = []
    for item in range(class_ref.shape[0]):
        owner = lax.div(class_ref[item], class_local)
        rank = count_ref[owner]
        count_ref[owner] = rank + 1
        copy = pltpu.make_async_copy(image_ref.at[item], slot_ref.at[owner * 2 + rank], sems.at[item])
        copy.start()
        copies.append(copy)
    for copy in copies:
        copy.wait()


def place_slots(class_of, particles, owners, class_local):
    count, side, _ = particles.shape
    return pl.pallas_call(
        functools.partial(scatter_kernel, class_local),
        out_shape=jax.ShapeDtypeStruct((owners * 2, side, side), jnp.float32),
        in_specs=[pl.BlockSpec(memory_space=pltpu.SMEM), pl.BlockSpec(memory_space=pl.ANY)],
        out_specs=pl.BlockSpec(memory_space=pl.ANY),
        scratch_shapes=[pltpu.SMEM((owners,), jnp.int32), pltpu.SemaphoreType.DMA((count,))],
        name="place_slots",
    )(class_of, particles)


def pair_step(source, block_at, info_ref, image_ref, ref_ref, contrast_ref, turn_ref, best_ref, left_ref,
              right_high_ref, right_low_ref, col_ref, row_ref, score_ref, numer_ref):
    side = image_ref.shape[-1]
    turns = [info_ref[1, 2 * source + k] for k in range(2)]
    highs, lows = [], []
    for k in range(2):
        image = image_ref[block_at, k]
        odd = lax.rem(turns[k], 2) == 1
        image = jnp.where(odd, image.T, image)
        high, low = split(image)
        highs.append(high)
        lows.append(low)
    stacked = jnp.concatenate(
        [jnp.concatenate(highs, axis=1), jnp.concatenate(lows, axis=1)], axis=0
    )
    halfway = jnp.dot(left_ref[...], stacked, preferred_element_type=jnp.float32)
    halfway = halfway[: 2 * HALF] + halfway[2 * HALF :]
    parts = []
    for k in range(2):
        sign = jnp.where(lax.rem(turns[k], 2) == 1, -1.0, 1.0).astype(jnp.float32)
        lanes = slice(k * side, (k + 1) * side)
        parts.append(jnp.concatenate([halfway[:HALF, lanes], sign * halfway[HALF:, lanes]], axis=1))
    high, low = split(jnp.concatenate(parts, axis=0))
    spectrum = (
        jnp.dot(high, right_high_ref[...], preferred_element_type=jnp.float32)
        + jnp.dot(low, right_high_ref[...], preferred_element_type=jnp.float32)
        + jnp.dot(high, right_low_ref[...], preferred_element_type=jnp.float32)
    )
    products = []
    filtered = []
    for k in range(2):
        slot = 2 * source + k
        rows = slice(k * HALF, (k + 1) * HALF)
        sign = jnp.where(turns[k] >= 2, -1.0, 1.0).astype(jnp.float32)
        real = spectrum[rows, :side]
        imag = sign * spectrum[rows, side:]
        turn = turn_ref[turns[k]]
        contrast = contrast_ref[info_ref[3, slot]]
        turn_real, turn_imag = turn[:, :side], turn[:, side:]
        filt_real = contrast * (real * turn_real - imag * turn_imag)
        filt_imag = contrast * (real * turn_imag + imag * turn_real)
        filtered.append((filt_real, filt_imag))
        ref = ref_ref[info_ref[0, slot]]
        ref_real, ref_imag = ref[:, :side], ref[:, side:]
        products.append(
            jnp.concatenate(
                [
                    filt_real * ref_real + filt_imag * ref_imag,
                    filt_imag * ref_real - filt_real * ref_imag,
                ],
                axis=1,
            )
        )
    high, low = split(jnp.concatenate(products, axis=0))
    by_col = jnp.dot(high, col_ref[...], preferred_element_type=jnp.float32)
    by_col = (
        by_col[:, :side]
        + by_col[:, side:]
        + jnp.dot(low, col_ref[:, :side], preferred_element_type=jnp.float32)
    )
    sums = []
    for k in range(2):
        total = jnp.sum(by_col[k * HALF : (k + 1) * HALF] * row_ref[...], axis=0, keepdims=True)
        sums.append(total + pltpu.roll(total, side // 2, axis=1))
    lane = lax.broadcasted_iota(jnp.int32, (1, side), 1)
    score_ref[pl.ds(source, 1), :] = jnp.where(lane < side // 2, sums[0], sums[1])
    for k in range(2):
        slot = 2 * source + k

        @pl.when(info_ref[4, slot] > 0)
        def _(k=k, slot=slot):
            best = best_ref[info_ref[2, slot]]
            best_real, best_imag = best[:, :side], best[:, side:]
            filt_real, filt_imag = filtered[k]
            local = info_ref[0, slot]
            numer_ref[local, :, :side] += filt_real * best_real - filt_imag * best_imag
            numer_ref[local, :, side:] += filt_real * best_imag + filt_imag * best_real


def owner_kernel(step_sources, info_ref, image_ref, *refs):
    numer_ref = refs[-1]

    @pl.when(pl.program_id(0) == 0)
    def _():
        numer_ref[...] = jnp.zeros_like(numer_ref)

    for at in range(step_sources):
        pair_step(pl.program_id(0) * step_sources + at, at, info_ref, image_ref, *refs)


def owner_terms(info, images, refs, contrast, turn, best, left, right_high, right_low, col, row):
    sources, _, side, _ = images.shape
    step_sources = 4
    whole = lambda x: pl.BlockSpec(x.shape, lambda i: (0,) * x.ndim)
    tables = (refs, contrast, turn, best, left, right_high, right_low, col, row)
    return pl.pallas_call(
        functools.partial(owner_kernel, step_sources),
        grid=(sources // step_sources,),
        out_shape=(
            jax.ShapeDtypeStruct((sources, side), jnp.float32),
            jax.ShapeDtypeStruct((refs.shape[0], HALF, 2 * side), jnp.float32),
        ),
        in_specs=[
            pl.BlockSpec(memory_space=pltpu.SMEM),
            pl.BlockSpec((step_sources, 2, side, side), lambda i: (i, 0, 0, 0)),
        ]
        + [whole(table) for table in tables],
        out_specs=(
            pl.BlockSpec((sources, side), lambda i: (0, 0)),
            pl.BlockSpec((refs.shape[0], HALF, 2 * side), lambda i: (0, 0, 0)),
        ),
        compiler_params=pltpu.CompilerParams(vmem_limit_bytes=40 * MIB),
        name="owner_terms",
    )(info, images, *tables)


def finish_kernel(a_ref, b_ref, c_ref, d_ref, denom_ref, lanes_ref, unfold_ref, out_ref):
    side = out_ref.shape[-1]
    for at in range(out_ref.shape[0]):
        total = (a_ref[at] + b_ref[at]) + (c_ref[at] + d_ref[at])
        for part in range(2):
            ratio = total[:, part * side : (part + 1) * side] / denom_ref[at]
            back = jnp.dot(
                ratio, lanes_ref[...], precision=lax.Precision.HIGHEST, preferred_element_type=jnp.float32
            )
            back = jnp.dot(
                unfold_ref[...], back, precision=lax.Precision.HIGHEST, preferred_element_type=jnp.float32
            )
            out_ref[at, part, : side // 2] = ratio[: side // 2]
            out_ref[at, part, side // 2 :] = back if part == 0 else -back


def finish(blocks, denom, lanes, unfold, side):
    return pl.pallas_call(
        finish_kernel,
        out_shape=jax.ShapeDtypeStruct((denom.shape[0], 2, side, side), jnp.float32),
        compiler_params=pltpu.CompilerParams(vmem_limit_bytes=16 * MIB),
        name="finish",
    )(*blocks, denom, lanes, unfold)


def body(
    particles, references, class_of, rotation_bin, shift_best, defocus_bin, shift_list,
    defocus, chips_y,
):
    side = particles.shape[-1]
    class_local = references.shape[0]
    bins = defocus.shape[0]
    owners = lax.axis_size("cls")
    groups = lax.axis_size("grp")
    me_cls, me_grp = lax.axis_index("cls"), lax.axis_index("grp")
    unit = 2.0 * math.pi / side

    send = place_slots(class_of, particles, owners, class_local)
    images = lax.all_to_all(
        send.reshape(owners, 2, side, side), "cls", split_axis=0, concat_axis=0, tiled=True
    )

    ints = jnp.stack([class_of, rotation_bin, shift_best, defocus_bin])[None]
    everyone = lax.all_gather(ints, ("grp", "cls"), axis=0, tiled=True)

    group = lax.dynamic_slice_in_dim(everyone, me_grp * owners, owners, 0)
    mine = group[:, 0] // class_local == me_cls
    rank = jnp.cumsum(mine.astype(jnp.int32), axis=1) - 1
    chosen = mine[:, None, :] & (rank[:, None, :] == jnp.arange(2, dtype=jnp.int32)[None, :, None])
    fields = jnp.stack(
        [group[:, 0] % class_local, group[:, 1], group[:, 2], group[:, 3], jnp.ones_like(group[:, 0])]
    )
    info = jnp.sum(jnp.where(chosen[None], fields[:, :, None, :], 0), axis=-1).reshape(5, 2 * owners)

    own_classes = class_local // groups
    own = me_cls * class_local + me_grp * own_classes + jnp.arange(own_classes, dtype=jnp.int32)
    flat_class = everyone[:, 0].reshape(-1)
    flat_bin = everyone[:, 3].reshape(-1)
    counts = jnp.sum(
        (
            (flat_class[None, None, :] == own[:, None, None])
            & (flat_bin[None, None, :] == jnp.arange(bins, dtype=jnp.int32)[None, :, None])
        ).astype(jnp.float32),
        axis=-1,
    )

    pixel = jnp.arange(side, dtype=jnp.int32)
    signed = jnp.where(pixel < side // 2, pixel, pixel - side).astype(jnp.float32)
    half = jnp.arange(HALF, dtype=jnp.int32)
    half_signed = jnp.where(half < side // 2, half, half - side).astype(jnp.float32)
    radius = (half_signed[:, None] ** 2 + signed[None, :] ** 2) / float((side // 2) ** 2)
    angle = defocus[:, None, None] * radius[None]
    contrast = -(0.995 * jnp.sin(angle) + 0.1 * jnp.cos(angle))
    denom = 1.0 + jnp.sum(counts[:, :, None, None] * (contrast * contrast)[None], axis=1)

    row_angle = ((half[None, :] * shift_list[:, 0][:, None]) % side).astype(jnp.float32) * unit
    col_angle = ((pixel[None, :] * shift_list[:, 1][:, None]) % side).astype(jnp.float32) * unit
    row_cos, row_sin = jnp.cos(row_angle), jnp.sin(row_angle)
    col_cos, col_sin = jnp.cos(col_angle), jnp.sin(col_angle)
    best = jnp.concatenate(
        [
            row_cos[:, :, None] * col_cos[:, None, :] - row_sin[:, :, None] * col_sin[:, None, :],
            row_sin[:, :, None] * col_cos[:, None, :] + row_cos[:, :, None] * col_sin[:, None, :],
        ],
        axis=2,
    )
    col = jnp.concatenate(
        [
            jnp.concatenate([col_cos.T, col_sin.T], axis=1),
            jnp.concatenate([-col_sin.T, col_cos.T], axis=1),
        ],
        axis=0,
    )
    col_high = lax.reduce_precision(col, exponent_bits=8, mantissa_bits=7)
    col = jnp.concatenate([col_high, col - col_high], axis=1).astype(jnp.bfloat16)
    row = jnp.concatenate([row_cos.T, -row_sin.T], axis=1) / side

    lanes, fold, unfold = flip_constants(side)
    live_rows = (half <= side // 2).astype(jnp.float32)[:, None]
    folded = jnp.einsum("ua,ciab->ciub", fold, references, precision=lax.Precision.HIGH)
    folded = jnp.einsum("ciub,bv->ciuv", folded, lanes, precision=lax.Precision.HIGH)
    top = references[:, :, :HALF] * live_rows
    refs = jnp.concatenate([top[:, 0] + folded[:, 0], top[:, 1] - folded[:, 1]], axis=2)

    left, right_high, right_low = dft_constants(side)
    slot_scores, numer = owner_terms(
        info, images, refs, contrast, jnp.asarray(turn_constants(side)), best, jnp.asarray(left),
        jnp.asarray(right_high), jnp.asarray(right_low), col, row,
    )

    cores = groups // chips_y
    core, me_y = me_grp % cores, me_grp // cores
    parts = numer.reshape(chips_y, cores, own_classes, HALF, 2 * side)
    keep = lax.dynamic_index_in_dim(parts, core, 1, keepdims=False)
    give = lax.dynamic_index_in_dim(parts, 1 - core, 1, keepdims=False)
    got = lax.ppermute(give, "grp", [(i, i ^ 1) for i in range(groups)])
    chip = keep + got
    blocks = [lax.dynamic_index_in_dim(chip, me_y, 0, keepdims=False)]
    for step in range(1, chips_y):
        block = lax.dynamic_index_in_dim(chip, (me_y + step) % chips_y, 0, keepdims=False)
        blocks.append(
            lax.ppermute(
                block,
                "grp",
                [(i, ((i // cores + step) % chips_y) * cores + i % cores) for i in range(groups)],
            )
        )

    home = lax.all_to_all(
        slot_scores.reshape(owners, 1, side), "cls", split_axis=0, concat_axis=0, tiled=True
    ).reshape(2 * owners, side // 2)
    owner_of = class_of // class_local
    earlier = jnp.tril(owner_of[:, None] == owner_of[None, :], -1)
    target = owner_of * 2 + jnp.sum(earlier.astype(jnp.int32), axis=1)
    scores = home[target]

    fresh_refs = finish(blocks, denom, jnp.asarray(lanes), jnp.asarray(unfold), side)
    return (scores, fresh_refs)


def solution(mesh):
    chips_y = mesh.shape["grp"] // 2
    return jax.shard_map(
        functools.partial(body, chips_y=chips_y),
        mesh=mesh,
        in_specs=(
            P(("grp", "cls"), None, None),
            P("cls", None, None, None),
            P(("grp", "cls")),
            P(("grp", "cls")),
            P(("grp", "cls")),
            P(("grp", "cls")),
            P(),
            P(),
        ),
        out_specs=(P(("grp", "cls"), None), P(("cls", "grp"), None, None, None)),
        check_vma=False,
    )
```

```python
import functools
import math

import jax
import jax.numpy as jnp
import numpy as np
from jax import lax
from jax.experimental import pallas as pl
from jax.experimental.pallas import tpu as pltpu
from jax.sharding import PartitionSpec as P

HALF = 72
TAG = 8
COUNT = HALF - 1
MIB = 1 << 20


def split_np(table):
    high = table.astype(jnp.bfloat16)
    low = (table - high.astype(np.float32)).astype(jnp.bfloat16)
    return high, low


def split(values):
    high = values.astype(jnp.bfloat16)
    low = (values - high.astype(jnp.float32)).astype(jnp.bfloat16)
    return high, low


def dft_constants(side):
    grid = np.outer(np.arange(side), np.arange(side)) % side
    angles = grid * (2.0 * np.pi / side)
    cos_table = (np.cos(angles) / np.sqrt(side)).astype(np.float32)
    sin_table = (np.sin(angles) / np.sqrt(side)).astype(np.float32)
    rows = side // 2 + 1
    left = np.zeros((2, HALF, side), np.float32)
    left[0, :rows] = cos_table[:rows]
    left[1, :rows] = sin_table[:rows]
    left_high, left_low = split_np(left.reshape(2 * HALF, side))
    left_table = np.concatenate(
        [
            np.concatenate([left_high, left_high], axis=1),
            np.concatenate([left_low, np.zeros_like(left_low)], axis=1),
        ],
        axis=0,
    )
    right = np.block([[cos_table, -sin_table], [-sin_table, -cos_table]]).astype(np.float32)
    right_high, right_low = split_np(right)
    return left_table, np.concatenate([right_high, right_high, right_low], axis=0)


def turn_constants(side):
    row = np.arange(HALF)[:, None] + 0 * np.arange(side)[None, :]
    col = 0 * np.arange(HALF)[:, None] + np.arange(side)[None, :]
    shifts = np.stack([0 * row, row, row + col, col]) % side
    angles = shifts * (2.0 * np.pi / side)
    return np.concatenate([np.cos(angles), np.sin(angles)], axis=2).astype(np.float32)


def flip_constants(side):
    lanes = np.zeros((side, side), np.float32)
    lanes[(-np.arange(side)) % side, np.arange(side)] = 1.0
    fold = np.zeros((HALF, side), np.float32)
    for u in range(1, side // 2):
        fold[u, side - u] = 1.0
    unfold = np.zeros((side // 2, HALF), np.float32)
    for r in range(side // 2):
        unfold[r, side // 2 - r] = 1.0
    return lanes, fold, unfold


def scatter_kernel(class_local, class_ref, turn_ref, shift_ref, bin_ref, image_ref, slot_ref,
                   count_ref, hold_ref, tag_ref, in_sems, out_sems, tag_sem):
    items, side, _ = hold_ref.shape
    loads = []
    for item in range(items):
        load = pltpu.make_async_copy(image_ref.at[item], hold_ref.at[item], in_sems.at[item])
        load.start()
        loads.append(load)
    for owner in range(count_ref.shape[0]):
        count_ref[owner] = 0
    tag_ref[...] = jnp.zeros_like(tag_ref)
    lane = lax.broadcasted_iota(jnp.int32, (1, side), 1)
    stores = []
    for item in range(items):
        owner = lax.div(class_ref[item], class_local)
        rank = count_ref[owner]
        count_ref[owner] = rank + 1
        loads[item].wait()
        store = pltpu.make_async_copy(
            hold_ref.at[item],
            slot_ref.at[owner, pl.ds(pl.multiple_of(rank * side, side), side), :],
            out_sems.at[item],
        )
        store.start()
        stores.append(store)
        fields = (class_ref[item] - owner * class_local, turn_ref[item], shift_ref[item], bin_ref[item], 1)
        tag = jnp.zeros((1, side), jnp.int32)
        for at, value in enumerate(fields):
            tag = jnp.where(lane == at, value, tag)
        tag_ref[owner, pl.ds(rank, 1), :] = tag.astype(jnp.float32)
    store = pltpu.make_async_copy(tag_ref, slot_ref.at[:, pl.ds(2 * side, TAG), :], tag_sem)
    store.start()
    stores.append(store)
    for store in stores:
        store.wait()


def place_slots(particles, class_of, rotation_bin, shift_best, defocus_bin, owners, class_local):
    count, side, _ = particles.shape
    return pl.pallas_call(
        functools.partial(scatter_kernel, class_local),
        out_shape=jax.ShapeDtypeStruct((owners, 2 * side + TAG, side), jnp.float32),
        in_specs=[pl.BlockSpec(memory_space=pltpu.SMEM)] * 4 + [pl.BlockSpec(memory_space=pltpu.HBM)],
        out_specs=pl.BlockSpec(memory_space=pltpu.HBM),
        scratch_shapes=[
            pltpu.SMEM((owners,), jnp.int32),
            pltpu.VMEM((count, side, side), jnp.float32),
            pltpu.VMEM((owners, TAG, side), jnp.float32),
            pltpu.SemaphoreType.DMA((count,)),
            pltpu.SemaphoreType.DMA((count,)),
            pltpu.SemaphoreType.DMA,
        ],
        compiler_params=pltpu.CompilerParams(vmem_limit_bytes=16 * MIB),
        name="place_slots",
    )(class_of, rotation_bin, shift_best, defocus_bin, particles)


def spectrum_kernel(step_sources, info_ref, image_ref, contrast_ref, turn_ref, best_ref, left_ref, right_ref,
                    keep_ref, give_ref, filt_ref, numer_ref, sems):
    side = image_ref.shape[-1]
    first = pl.program_id(0) * step_sources * 2
    lane = lax.broadcasted_iota(jnp.int32, (1, side), 1)

    @pl.when(pl.program_id(0) == 0)
    def _():
        numer_ref[...] = jnp.zeros_like(numer_ref)

    turns = [info_ref[1, first + item] for item in range(2 * step_sources)]
    parts = []
    for at in range(step_sources):
        highs, lows = [], []
        for k in range(2):
            image = image_ref[at, k * side : (k + 1) * side]
            odd = lax.rem(turns[2 * at + k], 2) == 1
            high, low = split(jnp.where(odd, image.T, image))
            highs.append(high)
            lows.append(low)
        stacked = jnp.concatenate(
            [jnp.concatenate(highs, axis=1), jnp.concatenate(lows, axis=1)], axis=0
        )
        halfway = jnp.dot(left_ref[...], stacked, preferred_element_type=jnp.float32)
        halfway = halfway[: 2 * HALF] + halfway[2 * HALF :]
        for k in range(2):
            odd = lax.rem(turns[2 * at + k], 2) == 1
            sign = jnp.where(odd, -1.0, 1.0).astype(jnp.float32)
            lanes = slice(k * side, (k + 1) * side)
            parts.append(
                jnp.concatenate([halfway[:HALF, lanes], sign * halfway[HALF:, lanes]], axis=1)
            )
    high, low = split(jnp.concatenate(parts, axis=0))
    spectrum = jnp.dot(
        jnp.concatenate([high, low, high], axis=1), right_ref[...], preferred_element_type=jnp.float32
    )
    for item in range(2 * step_sources):
        slot = first + item
        rows = slice(item * HALF, (item + 1) * HALF)
        sign = jnp.where(turns[item] >= 2, -1.0, 1.0).astype(jnp.float32)
        real = spectrum[rows, :side]
        imag = sign * spectrum[rows, side:]
        turn = turn_ref[turns[item]]
        contrast = contrast_ref[info_ref[3, slot]]
        turn_real, turn_imag = turn[:, :side], turn[:, side:]
        filt_real = contrast * (real * turn_real - imag * turn_imag)
        filt_imag = contrast * (real * turn_imag + imag * turn_real)
        filt_ref[item, :, :side] = filt_real
        filt_ref[item, :, side:] = filt_imag

        @pl.when(info_ref[4, slot] > 0)
        def _(slot=slot, filt_real=filt_real, filt_imag=filt_imag):
            best = best_ref[info_ref[2, slot]]
            best_real, best_imag = best[:, :side], best[:, side:]
            target = info_ref[5, slot]
            numer_ref[target, :, :side] += filt_real * best_real - filt_imag * best_imag
            numer_ref[target, :, side:] += filt_real * best_imag + filt_imag * best_real
            hit = (lane == info_ref[3, slot]).astype(jnp.float32)
            numer_ref[target, COUNT : COUNT + 1, :side] += hit

    @pl.when(pl.program_id(0) == pl.num_programs(0) - 1)
    def _():
        half = numer_ref.shape[0] // 2
        copies = [
            pltpu.make_async_copy(numer_ref.at[pl.ds(half, half)], give_ref, sems.at[0]),
            pltpu.make_async_copy(numer_ref.at[pl.ds(0, half)], keep_ref, sems.at[1]),
        ]
        for copy in copies:
            copy.start()
        for copy in copies:
            copy.wait()


def score_kernel(step_sources, info_ref, filt_ref, ref_ref, col_ref, row_ref, score_ref):
    side = score_ref.shape[-1]
    first = pl.program_id(0) * step_sources * 2
    products = []
    for item in range(2 * step_sources):
        ref = ref_ref[info_ref[0, first + item]]
        ref_real, ref_imag = ref[:, :side], ref[:, side:]
        filt_real, filt_imag = filt_ref[item, :, :side], filt_ref[item, :, side:]
        products.append(
            jnp.concatenate(
                [
                    filt_real * ref_real + filt_imag * ref_imag,
                    filt_imag * ref_real - filt_real * ref_imag,
                ],
                axis=1,
            )
        )
    high, low = split(jnp.concatenate(products, axis=0))
    by_col = jnp.dot(
        jnp.concatenate([high, low], axis=1), col_ref[...], preferred_element_type=jnp.float32
    )
    by_col = by_col[:, :side] + by_col[:, side:]
    lane = lax.broadcasted_iota(jnp.int32, (1, side), 1)
    for at in range(step_sources):
        sums = []
        for k in range(2):
            item = 2 * at + k
            total = jnp.sum(
                by_col[item * HALF : (item + 1) * HALF] * row_ref[...], axis=0, keepdims=True
            )
            sums.append(total + pltpu.roll(total, side // 2, axis=1))
        score_ref[at] = jnp.where(lane < side // 2, sums[0], sums[1])


def owner_spectra(info, images, contrast, turn, best, left, right, class_local):
    sources, _, side = images.shape
    step_sources = 4
    whole = lambda x: pl.BlockSpec(x.shape, lambda i: (0,) * x.ndim)
    tables = (contrast, turn, best, left, right)
    half = jax.ShapeDtypeStruct((class_local // 2, HALF, 2 * side), jnp.float32)
    return pl.pallas_call(
        functools.partial(spectrum_kernel, step_sources),
        grid=(sources // step_sources,),
        out_shape=(
            half,
            half,
            jax.ShapeDtypeStruct((2 * sources, HALF, 2 * side), jnp.float32),
        ),
        in_specs=[
            pl.BlockSpec(memory_space=pltpu.SMEM),
            pl.BlockSpec((step_sources, 2 * side, side), lambda i: (i, 0, 0)),
        ]
        + [whole(table) for table in tables],
        out_specs=(
            pl.BlockSpec(memory_space=pltpu.HBM),
            pl.BlockSpec(memory_space=pltpu.HBM),
            pl.BlockSpec((2 * step_sources, HALF, 2 * side), lambda i: (i, 0, 0)),
        ),
        scratch_shapes=[
            pltpu.VMEM((class_local, HALF, 2 * side), jnp.float32),
            pltpu.SemaphoreType.DMA((2,)),
        ],
        compiler_params=pltpu.CompilerParams(vmem_limit_bytes=32 * MIB),
        name="owner_spectra",
    )(info, images, *tables)


def owner_scores(info, filtered, refs, col, row):
    items, _, wide = filtered.shape
    step_sources = 4
    whole = lambda x: pl.BlockSpec(x.shape, lambda i: (0,) * x.ndim)
    return pl.pallas_call(
        functools.partial(score_kernel, step_sources),
        grid=(items // 2 // step_sources,),
        out_shape=jax.ShapeDtypeStruct((items // 2, 1, wide // 2), jnp.float32),
        in_specs=[
            pl.BlockSpec(memory_space=pltpu.SMEM),
            pl.BlockSpec((2 * step_sources, HALF, wide), lambda i: (i, 0, 0)),
            whole(refs), whole(col), whole(row),
        ],
        out_specs=pl.BlockSpec((step_sources, 1, wide // 2), lambda i: (i, 0, 0)),
        compiler_params=pltpu.CompilerParams(vmem_limit_bytes=24 * MIB),
        name="owner_scores",
    )(info, filtered, refs, col, row)


def finish_kernel(mine_ref, a_ref, b_ref, c_ref, square_ref, lanes_ref, unfold_ref, out_ref):
    side = out_ref.shape[-1]
    for at in range(out_ref.shape[0]):
        total = (mine_ref[at] + a_ref[at]) + (b_ref[at] + c_ref[at])
        weight = jnp.zeros((HALF, side), jnp.float32)
        for which in range(square_ref.shape[0]):
            weight += total[COUNT : COUNT + 1, which : which + 1] * square_ref[which]
        inverse = 1.0 / (weight + 1.0)
        for part in range(2):
            ratio = total[:, part * side : (part + 1) * side] * inverse
            back = jnp.dot(
                ratio, lanes_ref[...], precision=lax.Precision.HIGHEST, preferred_element_type=jnp.float32
            )
            back = jnp.dot(
                unfold_ref[...], back, precision=lax.Precision.HIGHEST, preferred_element_type=jnp.float32
            )
            out_ref[at, part, : side // 2] = ratio[: side // 2]
            out_ref[at, part, side // 2 :] = back if part == 0 else -back


def finish(blocks, square, lanes, unfold, side):
    return pl.pallas_call(
        finish_kernel,
        out_shape=jax.ShapeDtypeStruct((blocks[0].shape[0], 2, side, side), jnp.float32),
        compiler_params=pltpu.CompilerParams(vmem_limit_bytes=16 * MIB),
        name="finish",
    )(*blocks, square, lanes, unfold)


def pick_kernel(target_ref, home_ref, out_ref):
    items, shifts = out_ref.shape
    for item in range(items):
        target = target_ref[item]
        row = home_ref[lax.div(target, 2)]
        row = jnp.where(lax.rem(target, 2) == 1, pltpu.roll(row, shifts, axis=1), row)
        out_ref[item : item + 1, :] = row[:, :shifts]


def pick(target, home):
    return pl.pallas_call(
        pick_kernel,
        out_shape=jax.ShapeDtypeStruct((target.shape[0], home.shape[-1] // 2), jnp.float32),
        in_specs=[pl.BlockSpec(memory_space=pltpu.SMEM), pl.BlockSpec(memory_space=pltpu.VMEM)],
        compiler_params=pltpu.CompilerParams(vmem_limit_bytes=16 * MIB),
        name="pick",
    )(target, home)


def body(
    particles, references, class_of, rotation_bin, shift_best, defocus_bin, shift_list,
    defocus, chips_y,
):
    side = particles.shape[-1]
    class_local = references.shape[0]
    owners = lax.axis_size("cls")
    groups = lax.axis_size("grp")
    me_grp = lax.axis_index("grp")
    unit = 2.0 * math.pi / side

    send = place_slots(
        particles, class_of, rotation_bin, shift_best, defocus_bin, owners, class_local
    )
    images = lax.all_to_all(send, "cls", split_axis=0, concat_axis=0, tiled=True)

    cores = groups // chips_y
    core, me_y = me_grp % cores, me_grp // cores
    own_classes = class_local // groups
    tags = images[:, 2 * side : 2 * side + 2, :5].astype(jnp.int32).reshape(2 * owners, 5)
    local = tags[:, 0]
    place = local // own_classes
    target = (
        ((place % cores - core) % cores) * chips_y + (place // cores - me_y) % chips_y
    ) * own_classes + local % own_classes
    info = jnp.concatenate([tags, target[:, None]], axis=1).T

    pixel = jnp.arange(side, dtype=jnp.int32)
    signed = jnp.where(pixel < side // 2, pixel, pixel - side).astype(jnp.float32)
    half = jnp.arange(HALF, dtype=jnp.int32)
    half_signed = jnp.where(half < side // 2, half, half - side).astype(jnp.float32)
    radius = (half_signed[:, None] ** 2 + signed[None, :] ** 2) / float((side // 2) ** 2)
    angle = defocus[:, None, None] * radius[None]
    contrast = -(0.995 * jnp.sin(angle) + 0.1 * jnp.cos(angle))

    row_angle = ((half[None, :] * shift_list[:, 0][:, None]) % side).astype(jnp.float32) * unit
    col_angle = ((pixel[None, :] * shift_list[:, 1][:, None]) % side).astype(jnp.float32) * unit
    row_cos, row_sin = jnp.cos(row_angle), jnp.sin(row_angle)
    col_cos, col_sin = jnp.cos(col_angle), jnp.sin(col_angle)
    best = jnp.concatenate(
        [
            row_cos[:, :, None] * col_cos[:, None, :] - row_sin[:, :, None] * col_sin[:, None, :],
            row_sin[:, :, None] * col_cos[:, None, :] + row_cos[:, :, None] * col_sin[:, None, :],
        ],
        axis=2,
    )
    col = jnp.concatenate(
        [
            jnp.concatenate([col_cos.T, col_sin.T], axis=1),
            jnp.concatenate([-col_sin.T, col_cos.T], axis=1),
        ],
        axis=0,
    )
    col_high = lax.reduce_precision(col, exponent_bits=8, mantissa_bits=7)
    col = jnp.concatenate([col_high, col - col_high], axis=1).astype(jnp.bfloat16)
    col = jnp.concatenate([col, col], axis=0)
    row = jnp.concatenate([row_cos.T, -row_sin.T], axis=1) / side

    lanes, fold, unfold = flip_constants(side)
    live_rows = (half <= side // 2).astype(jnp.float32)[:, None]
    folded = jnp.einsum("ua,ciab->ciub", fold, references, precision=lax.Precision.HIGH)
    folded = jnp.einsum("ciub,bv->ciuv", folded, lanes, precision=lax.Precision.HIGH)
    top = references[:, :, :HALF] * live_rows
    refs = jnp.concatenate([top[:, 0] + folded[:, 0], top[:, 1] - folded[:, 1]], axis=2)

    left, right = dft_constants(side)
    keep, give, filtered = owner_spectra(
        info, images, contrast, jnp.asarray(turn_constants(side)), best, jnp.asarray(left),
        jnp.asarray(right), class_local,
    )
    slot_scores = owner_scores(info, filtered, refs, col, row)

    got = lax.ppermute(give, "grp", [(i, i ^ 1) for i in range(groups)])
    blocks = []
    for step in range(chips_y):
        part = slice(step * own_classes, (step + 1) * own_classes)
        block = keep[part] + got[part]
        pairs = [(i, ((i // cores + step) % chips_y) * cores + i % cores) for i in range(groups)]
        blocks.append(lax.ppermute(block, "grp", pairs) if step else block)

    home = lax.all_to_all(slot_scores, "cls", split_axis=0, concat_axis=0, tiled=True)
    owner_of = class_of // class_local
    earlier = jnp.tril(owner_of[:, None] == owner_of[None, :], -1)
    scores = pick(owner_of * 2 + jnp.sum(earlier.astype(jnp.int32), axis=1), home)

    fresh_refs = finish(
        blocks, contrast * contrast, jnp.asarray(lanes), jnp.asarray(unfold), side
    )
    return (scores, fresh_refs)


def solution(mesh):
    chips_y = mesh.shape["grp"] // 2
    return jax.shard_map(
        functools.partial(body, chips_y=chips_y),
        mesh=mesh,
        in_specs=(
            P(("grp", "cls"), None, None),
            P("cls", None, None, None),
            P(("grp", "cls")),
            P(("grp", "cls")),
            P(("grp", "cls")),
            P(("grp", "cls")),
            P(),
            P(),
        ),
        out_specs=(P(("grp", "cls"), None), P(("cls", "grp"), None, None, None)),
        check_vma=False,
    )
```

```python
import functools
import math

import jax
import jax.numpy as jnp
import numpy as np
from jax import lax
from jax.experimental import pallas as pl
from jax.experimental.pallas import tpu as pltpu
from jax.sharding import PartitionSpec as P

HALF = 72
TAG = 8
COUNT = HALF - 1
SHIFT = 8
MIB = 1 << 20


def split_np(table):
    high = table.astype(jnp.bfloat16)
    low = (table - high.astype(np.float32)).astype(jnp.bfloat16)
    return high, low


def split(values):
    high = values.astype(jnp.bfloat16)
    low = (values - high.astype(jnp.float32)).astype(jnp.bfloat16)
    return high, low


def dft_constants(side):
    grid = np.outer(np.arange(side), np.arange(side)) % side
    angles = grid * (2.0 * np.pi / side)
    cos_table = (np.cos(angles) / np.sqrt(side)).astype(np.float32)
    sin_table = (np.sin(angles) / np.sqrt(side)).astype(np.float32)
    rows = side // 2 + 1
    left = np.zeros((2, HALF, side), np.float32)
    left[0, :rows] = cos_table[:rows]
    left[1, :rows] = sin_table[:rows]
    left_high, left_low = split_np(left.reshape(2 * HALF, side))
    left_table = np.concatenate(
        [
            np.concatenate([left_high, left_high], axis=1),
            np.concatenate([left_low, np.zeros_like(left_low)], axis=1),
        ],
        axis=0,
    )
    right = np.block([[cos_table, -sin_table], [-sin_table, -cos_table]]).astype(np.float32)
    right_high, right_low = split_np(right)
    return left_table, np.concatenate([right_high, right_high, right_low], axis=0)


def turn_constants(side):
    row = np.arange(HALF)[:, None] + 0 * np.arange(side)[None, :]
    col = 0 * np.arange(HALF)[:, None] + np.arange(side)[None, :]
    shifts = np.stack([0 * row, row, row + col, col]) % side
    angles = shifts * (2.0 * np.pi / side)
    return np.concatenate([np.cos(angles), np.sin(angles)], axis=2).astype(np.float32)


def shift_constants(side):
    steps = np.arange(-SHIFT, SHIFT + 1)[:, None]
    row = np.broadcast_to((steps * np.arange(HALF) % side)[:, :, None], (2 * SHIFT + 1, HALF, side))
    col = (steps * np.arange(side) % side)[:, None, :]
    return [
        np.concatenate([np.cos(t * (2.0 * np.pi / side)), np.sin(t * (2.0 * np.pi / side))], axis=2).astype(np.float32)
        for t in (row, col)
    ]


def flip_constants(side):
    lanes = np.zeros((side, side), np.float32)
    lanes[(-np.arange(side)) % side, np.arange(side)] = 1.0
    fold = np.zeros((HALF, side), np.float32)
    for u in range(1, side // 2):
        fold[u, side - u] = 1.0
    unfold = np.zeros((side // 2, HALF), np.float32)
    for r in range(side // 2):
        unfold[r, side // 2 - r] = 1.0
    return lanes, fold, unfold


def scatter_kernel(class_local, chips_y, class_hbm, turn_hbm, best_hbm, bin_hbm, shift_hbm, image_ref, slot_ref,
                   class_ref, turn_ref, best_ref, bin_ref, shift_ref, count_ref, hold_ref, tag_ref,
                   int_sems, in_sems, out_sems, tag_sem):
    items, side, _ = hold_ref.shape
    pairs = ((class_hbm, class_ref), (turn_hbm, turn_ref), (best_hbm, best_ref), (bin_hbm, bin_ref), (shift_hbm, shift_ref))
    ints = [pltpu.make_async_copy(a, b, int_sems.at[at]) for at, (a, b) in enumerate(pairs)]
    for load in ints:
        load.start()
    loads = []
    for item in range(items):
        load = pltpu.make_async_copy(image_ref.at[item], hold_ref.at[item], in_sems.at[item])
        load.start()
        loads.append(load)
    for owner in range(count_ref.shape[0]):
        count_ref[owner] = 0
    tag_ref[...] = jnp.zeros_like(tag_ref)
    lane = lax.broadcasted_iota(jnp.int32, (1, side), 1)
    groups = lax.axis_size("grp")
    me_grp = lax.axis_index("grp")
    cores, own = groups // chips_y, class_local // groups
    core, me_y = lax.rem(me_grp, cores), lax.div(me_grp, cores)
    for load in ints:
        load.wait()
    stores = []
    for item in range(items):
        owner = lax.div(class_ref[item], class_local)
        local = class_ref[item] - owner * class_local
        rank = count_ref[owner]
        count_ref[owner] = rank + 1
        loads[item].wait()
        store = pltpu.make_async_copy(
            hold_ref.at[item],
            slot_ref.at[owner, pl.ds(pl.multiple_of(rank * side, side), side), :],
            out_sems.at[item],
        )
        store.start()
        stores.append(store)
        place = lax.div(local, own)
        other = lax.rem(lax.rem(place, cores) - core + cores, cores)
        step = lax.rem(lax.div(place, cores) - me_y + chips_y, chips_y)
        target = (other * chips_y + step) * own + lax.rem(local, own)
        best = best_ref[item]
        fields = (local, turn_ref[item], shift_ref[0, best] + SHIFT, shift_ref[1, best] + SHIFT, bin_ref[item], target, 1)
        tag = jnp.zeros((1, side), jnp.int32)
        for at, value in enumerate(fields):
            tag = jnp.where(lane == at, value, tag)
        tag_ref[owner, pl.ds(rank, 1), :] = tag.astype(jnp.float32)
    store = pltpu.make_async_copy(tag_ref, slot_ref.at[:, pl.ds(2 * side, TAG), :], tag_sem)
    store.start()
    stores.append(store)
    for store in stores:
        store.wait()


def place_slots(particles, class_of, rotation_bin, shift_best, defocus_bin, shift_list, owners, class_local, chips_y):
    count, side, _ = particles.shape
    return pl.pallas_call(
        functools.partial(scatter_kernel, class_local, chips_y),
        out_shape=jax.ShapeDtypeStruct((owners, 2 * side + TAG, side), jnp.float32),
        in_specs=[pl.BlockSpec(memory_space=pltpu.HBM)] * 6,
        out_specs=pl.BlockSpec(memory_space=pltpu.HBM),
        scratch_shapes=[pltpu.SMEM((count,), jnp.int32)] * 4
        + [
            pltpu.SMEM(shift_list.shape[::-1], jnp.int32),
            pltpu.SMEM((owners,), jnp.int32),
            pltpu.VMEM((count, side, side), jnp.float32),
            pltpu.VMEM((owners, TAG, side), jnp.float32),
            pltpu.SemaphoreType.DMA((5,)),
            pltpu.SemaphoreType.DMA((count,)),
            pltpu.SemaphoreType.DMA((count,)),
            pltpu.SemaphoreType.DMA,
        ],
        compiler_params=pltpu.CompilerParams(vmem_limit_bytes=58 * MIB),
        name="place_slots",
    )(class_of, rotation_bin, shift_best, defocus_bin, shift_list.T, particles)


def spectrum_kernel(step_sources, info_ref, image_ref, contrast_ref, turn_ref, row_ref, col_ref, left_ref, right_ref,
                    *refs):
    keep_ref, give_ref, filt_ref, numer_ref, sems = refs[-5:]
    side = image_ref.shape[-1]
    first = pl.program_id(0) * step_sources
    lane = lax.broadcasted_iota(jnp.int32, (1, side), 1)

    @pl.when(pl.program_id(0) == 0)
    def _():
        numer_ref[...] = jnp.zeros_like(numer_ref)

    turns = [info_ref[first + item // 2, item % 2, 1] for item in range(2 * step_sources)]
    parts = []
    for at in range(step_sources):
        highs, lows = [], []
        for k in range(2):
            image = image_ref[at, k * side : (k + 1) * side]
            odd = lax.rem(turns[2 * at + k], 2) == 1
            high, low = split(jnp.where(odd, image.T, image))
            highs.append(high)
            lows.append(low)
        stacked = jnp.concatenate(
            [jnp.concatenate(highs, axis=1), jnp.concatenate(lows, axis=1)], axis=0
        )
        halfway = jnp.dot(left_ref[...], stacked, preferred_element_type=jnp.float32)
        halfway = halfway[: 2 * HALF] + halfway[2 * HALF :]
        for k in range(2):
            odd = lax.rem(turns[2 * at + k], 2) == 1
            sign = jnp.where(odd, -1.0, 1.0).astype(jnp.float32)
            lanes = slice(k * side, (k + 1) * side)
            parts.append(
                jnp.concatenate([halfway[:HALF, lanes], sign * halfway[HALF:, lanes]], axis=1)
            )
    high, low = split(jnp.concatenate(parts, axis=0))
    spectrum = jnp.dot(
        jnp.concatenate([high, low, high], axis=1), right_ref[...], preferred_element_type=jnp.float32
    )
    for item in range(2 * step_sources):
        info = [info_ref[first + item // 2, item % 2, at] for at in range(7)]
        rows = slice(item * HALF, (item + 1) * HALF)
        sign = jnp.where(turns[item] >= 2, -1.0, 1.0).astype(jnp.float32)
        real = spectrum[rows, :side]
        imag = sign * spectrum[rows, side:]
        turn = turn_ref[turns[item]]
        contrast = contrast_ref[info[4]]
        turn_real, turn_imag = turn[:, :side], turn[:, side:]
        filt_real = contrast * (real * turn_real - imag * turn_imag)
        filt_imag = contrast * (real * turn_imag + imag * turn_real)
        filt_ref[item, :, :side] = filt_real
        filt_ref[item, :, side:] = filt_imag

        @pl.when(info[6] > 0)
        def _(info=info, filt_real=filt_real, filt_imag=filt_imag):
            target = info[5]
            row_real, row_imag = row_ref[info[2], :, :side], row_ref[info[2], :, side:]
            half_real = filt_real * row_real - filt_imag * row_imag
            half_imag = filt_real * row_imag + filt_imag * row_real
            col_real, col_imag = col_ref[info[3], :, :side], col_ref[info[3], :, side:]
            numer_ref[target, :, :side] += half_real * col_real - half_imag * col_imag
            numer_ref[target, :, side:] += half_real * col_imag + half_imag * col_real
            hit = (lane == info[4]).astype(jnp.float32)
            numer_ref[target, COUNT : COUNT + 1, :side] += hit

    @pl.when(pl.program_id(0) == pl.num_programs(0) - 1)
    def _():
        half = numer_ref.shape[0] // 2
        copies = [
            pltpu.make_async_copy(numer_ref.at[pl.ds(half, half)], give_ref, sems.at[0]),
            pltpu.make_async_copy(numer_ref.at[pl.ds(0, half)], keep_ref, sems.at[1]),
        ]
        for copy in copies:
            copy.start()
        for copy in copies:
            copy.wait()


def score_kernel(step_sources, info_ref, filt_ref, ref_ref, col_ref, row_ref, score_ref):
    side = score_ref.shape[-1]
    first = pl.program_id(0) * step_sources
    products = []
    for item in range(2 * step_sources):
        ref = ref_ref[info_ref[first + item // 2, item % 2, 0]]
        ref_real, ref_imag = ref[:, :side], ref[:, side:]
        filt_real, filt_imag = filt_ref[item, :, :side], filt_ref[item, :, side:]
        products.append(
            jnp.concatenate(
                [
                    filt_real * ref_real + filt_imag * ref_imag,
                    filt_imag * ref_real - filt_real * ref_imag,
                ],
                axis=1,
            )
        )
    high, low = split(jnp.concatenate(products, axis=0))
    by_col = jnp.dot(
        jnp.concatenate([high, low], axis=1), col_ref[...], preferred_element_type=jnp.float32
    )
    by_col = by_col[:, :side] + by_col[:, side:]
    lane = lax.broadcasted_iota(jnp.int32, (1, side), 1)
    for at in range(step_sources):
        sums = []
        for k in range(2):
            item = 2 * at + k
            total = jnp.sum(
                by_col[item * HALF : (item + 1) * HALF] * row_ref[...], axis=0, keepdims=True
            )
            sums.append(total + pltpu.roll(total, side // 2, axis=1))
        score_ref[at] = jnp.where(lane < side // 2, sums[0], sums[1])


def owner_spectra(info, images, contrast, turn, row, col, left, right, ready, class_local):
    sources, _, side = images.shape
    step_sources = 4
    whole = lambda x: pl.BlockSpec(x.shape, lambda i: (0,) * x.ndim)
    tables = (contrast, turn, row, col, left, right)
    half = jax.ShapeDtypeStruct((class_local // 2, HALF, 2 * side), jnp.float32)
    return pl.pallas_call(
        functools.partial(spectrum_kernel, step_sources),
        grid=(sources // step_sources,),
        out_shape=(
            half,
            half,
            jax.ShapeDtypeStruct((2 * sources, HALF, 2 * side), jnp.float32),
        ),
        in_specs=[
            pl.BlockSpec(memory_space=pltpu.SMEM),
            pl.BlockSpec((step_sources, 2 * side, side), lambda i: (i, 0, 0)),
        ]
        + [whole(table) for table in tables]
        + [pl.BlockSpec(memory_space=pl.ANY)] * len(ready),
        out_specs=(
            pl.BlockSpec(memory_space=pltpu.HBM),
            pl.BlockSpec(memory_space=pltpu.HBM),
            pl.BlockSpec((2 * step_sources, HALF, 2 * side), lambda i: (i, 0, 0)),
        ),
        scratch_shapes=[
            pltpu.VMEM((class_local, HALF, 2 * side), jnp.float32),
            pltpu.SemaphoreType.DMA((2,)),
        ],
        compiler_params=pltpu.CompilerParams(vmem_limit_bytes=24 * MIB),
        name="owner_spectra",
    )(info, images, *tables, *ready)


def owner_scores(info, filtered, refs, col, row):
    items, _, wide = filtered.shape
    step_sources = 4
    whole = lambda x: pl.BlockSpec(x.shape, lambda i: (0,) * x.ndim)
    return pl.pallas_call(
        functools.partial(score_kernel, step_sources),
        grid=(items // 2 // step_sources,),
        out_shape=jax.ShapeDtypeStruct((items // 2, 1, wide // 2), jnp.float32),
        in_specs=[
            pl.BlockSpec(memory_space=pltpu.SMEM),
            pl.BlockSpec((2 * step_sources, HALF, wide), lambda i: (i, 0, 0)),
            whole(refs), whole(col), whole(row),
        ],
        out_specs=pl.BlockSpec((step_sources, 1, wide // 2), lambda i: (i, 0, 0)),
        compiler_params=pltpu.CompilerParams(vmem_limit_bytes=24 * MIB),
        name="owner_scores",
    )(info, filtered, refs, col, row)


def finish_kernel(mine_ref, a_ref, b_ref, c_ref, contrast_ref, lanes_ref, unfold_ref, out_ref):
    side = out_ref.shape[-1]
    for at in range(out_ref.shape[0]):
        total = (mine_ref[at] + a_ref[at]) + (b_ref[at] + c_ref[at])
        weight = jnp.zeros((HALF, side), jnp.float32)
        for which in range(contrast_ref.shape[0]):
            contrast = contrast_ref[which]
            weight += total[COUNT : COUNT + 1, which : which + 1] * (contrast * contrast)
        inverse = 1.0 / (weight + 1.0)
        for part in range(2):
            ratio = total[:, part * side : (part + 1) * side] * inverse
            back = jnp.dot(
                ratio, lanes_ref[...], precision=lax.Precision.HIGHEST, preferred_element_type=jnp.float32
            )
            back = jnp.dot(
                unfold_ref[...], back, precision=lax.Precision.HIGHEST, preferred_element_type=jnp.float32
            )
            out_ref[at, part, : side // 2] = ratio[: side // 2]
            out_ref[at, part, side // 2 :] = back if part == 0 else -back


def finish(blocks, contrast, lanes, unfold, side):
    return pl.pallas_call(
        finish_kernel,
        out_shape=jax.ShapeDtypeStruct((blocks[0].shape[0], 2, side, side), jnp.float32),
        compiler_params=pltpu.CompilerParams(vmem_limit_bytes=16 * MIB),
        name="finish",
    )(*blocks, contrast, lanes, unfold)


def pick_kernel(target_ref, home_ref, out_ref):
    items, shifts = out_ref.shape
    for item in range(items):
        target = target_ref[item]
        row = home_ref[lax.div(target, 2)]
        row = jnp.where(lax.rem(target, 2) == 1, pltpu.roll(row, shifts, axis=1), row)
        out_ref[item : item + 1, :] = row[:, :shifts]


def pick(target, home):
    return pl.pallas_call(
        pick_kernel,
        out_shape=jax.ShapeDtypeStruct((target.shape[0], home.shape[-1] // 2), jnp.float32),
        in_specs=[pl.BlockSpec(memory_space=pltpu.SMEM), pl.BlockSpec(memory_space=pltpu.VMEM)],
        compiler_params=pltpu.CompilerParams(vmem_limit_bytes=16 * MIB),
        name="pick",
    )(target, home)


def body(
    particles, references, class_of, rotation_bin, shift_best, defocus_bin, shift_list,
    defocus, chips_y,
):
    side = particles.shape[-1]
    class_local = references.shape[0]
    owners = lax.axis_size("cls")
    groups = lax.axis_size("grp")
    unit = 2.0 * math.pi / side

    cores = groups // chips_y
    own_classes = class_local // groups

    send = place_slots(
        particles, class_of, rotation_bin, shift_best, defocus_bin, shift_list, owners, class_local, chips_y
    )
    images = lax.all_to_all(send, "cls", split_axis=0, concat_axis=0, tiled=True)

    pixel = jnp.arange(side, dtype=jnp.int32)
    signed = jnp.where(pixel < side // 2, pixel, pixel - side).astype(jnp.float32)
    half = jnp.arange(HALF, dtype=jnp.int32)
    half_signed = jnp.where(half < side // 2, half, half - side).astype(jnp.float32)
    radius = (half_signed[:, None] ** 2 + signed[None, :] ** 2) / float((side // 2) ** 2)
    angle = defocus[:, None, None] * radius[None]
    contrast = -(0.995 * jnp.sin(angle) + 0.1 * jnp.cos(angle))

    row_angle = ((half[None, :] * shift_list[:, 0][:, None]) % side).astype(jnp.float32) * unit
    col_angle = ((pixel[None, :] * shift_list[:, 1][:, None]) % side).astype(jnp.float32) * unit
    row_cos, row_sin = jnp.cos(row_angle), jnp.sin(row_angle)
    col_cos, col_sin = jnp.cos(col_angle), jnp.sin(col_angle)
    col = jnp.concatenate(
        [
            jnp.concatenate([col_cos.T, col_sin.T], axis=1),
            jnp.concatenate([-col_sin.T, col_cos.T], axis=1),
        ],
        axis=0,
    )
    col_high = lax.reduce_precision(col, exponent_bits=8, mantissa_bits=7)
    col = jnp.concatenate([col_high, col - col_high], axis=1).astype(jnp.bfloat16)
    col = jnp.concatenate([col, col], axis=0)
    row = jnp.concatenate([row_cos.T, -row_sin.T], axis=1) / side

    lanes, fold, unfold = flip_constants(side)
    live_rows = (half <= side // 2).astype(jnp.float32)[:, None]
    folded = jnp.einsum("ua,ciab->ciub", fold, references, precision=lax.Precision.HIGH)
    folded = jnp.einsum("ciub,bv->ciuv", folded, lanes, precision=lax.Precision.HIGH)
    top = references[:, :, :HALF] * live_rows
    refs = jnp.concatenate([top[:, 0] + folded[:, 0], top[:, 1] - folded[:, 1]], axis=2)

    refs = pltpu.with_memory_space_constraint(refs, pltpu.HBM)
    info = images[:, 2 * side : 2 * side + 2, :8].astype(jnp.int32)
    left, right = dft_constants(side)
    best_row, best_col = shift_constants(side)
    keep, give, filtered = owner_spectra(
        info, images, contrast, jnp.asarray(turn_constants(side)), jnp.asarray(best_row),
        jnp.asarray(best_col), jnp.asarray(left), jnp.asarray(right), (refs, col, row), class_local,
    )
    slot_scores = owner_scores(info, filtered, refs, col, row)

    got = lax.ppermute(give, "grp", [(i, i ^ 1) for i in range(groups)])
    got, slot_scores = lax.optimization_barrier((got, slot_scores))
    blocks = []
    for step in range(chips_y):
        part = slice(step * own_classes, (step + 1) * own_classes)
        block = keep[part] + got[part]
        pairs = [(i, ((i // cores + step) % chips_y) * cores + i % cores) for i in range(groups)]
        blocks.append(lax.ppermute(block, "grp", pairs) if step else block)

    home = lax.all_to_all(slot_scores, "cls", split_axis=0, concat_axis=0, tiled=True)
    fresh_refs = finish(
        blocks, contrast, jnp.asarray(lanes), jnp.asarray(unfold), side
    )
    home, fresh_refs = lax.optimization_barrier((home, fresh_refs))
    owner_of = class_of // class_local
    earlier = jnp.tril(owner_of[:, None] == owner_of[None, :], -1)
    scores = pick(owner_of * 2 + jnp.sum(earlier.astype(jnp.int32), axis=1), home)

    return (scores, fresh_refs)


def solution(mesh):
    chips_y = mesh.shape["grp"] // 2
    return jax.shard_map(
        functools.partial(body, chips_y=chips_y),
        mesh=mesh,
        in_specs=(
            P(("grp", "cls"), None, None),
            P("cls", None, None, None),
            P(("grp", "cls")),
            P(("grp", "cls")),
            P(("grp", "cls")),
            P(("grp", "cls")),
            P(),
            P(),
        ),
        out_specs=(P(("grp", "cls"), None), P(("cls", "grp"), None, None, None)),
        check_vma=False,
    )
```

```python
import functools
import math

import jax
import jax.numpy as jnp
import numpy as np
from jax import lax
from jax.experimental import pallas as pl
from jax.experimental.pallas import tpu as pltpu
from jax.sharding import PartitionSpec as P

HALF = 72
TAG = 8
COUNT = HALF - 1
SHIFT = 8
MIB = 1 << 20


def split_np(table):
    high = table.astype(jnp.bfloat16)
    low = (table - high.astype(np.float32)).astype(jnp.bfloat16)
    return high, low


def split(values):
    high = values.astype(jnp.bfloat16)
    low = (values - high.astype(jnp.float32)).astype(jnp.bfloat16)
    return high, low


def dft_constants(side):
    grid = np.outer(np.arange(side), np.arange(side)) % side
    angles = grid * (2.0 * np.pi / side)
    cos_table = (np.cos(angles) / np.sqrt(side)).astype(np.float32)
    sin_table = (np.sin(angles) / np.sqrt(side)).astype(np.float32)
    rows = side // 2 + 1
    left = np.zeros((2, HALF, side), np.float32)
    left[0, :rows] = cos_table[:rows]
    left[1, :rows] = sin_table[:rows]
    left_high, left_low = split_np(left.reshape(2 * HALF, side))
    left_table = np.concatenate(
        [
            np.concatenate([left_high, left_high], axis=1),
            np.concatenate([left_low, np.zeros_like(left_low)], axis=1),
        ],
        axis=0,
    )
    right = np.block([[cos_table, -sin_table], [-sin_table, -cos_table]]).astype(np.float32)
    right_high, right_low = split_np(right)
    return left_table, np.concatenate([right_high, right_high, right_low], axis=0)


def turn_constants(side):
    row = np.arange(HALF)[:, None] + 0 * np.arange(side)[None, :]
    col = 0 * np.arange(HALF)[:, None] + np.arange(side)[None, :]
    shifts = np.stack([0 * row, row, row + col, col]) % side
    angles = shifts * (2.0 * np.pi / side)
    return np.concatenate([np.cos(angles), np.sin(angles)], axis=2).astype(np.float32)


def shift_constants(side):
    steps = np.arange(-SHIFT, SHIFT + 1)[:, None]
    row = np.broadcast_to((steps * np.arange(HALF) % side)[:, :, None], (2 * SHIFT + 1, HALF, side))
    col = (steps * np.arange(side) % side)[:, None, :]
    return [
        np.concatenate([np.cos(t * (2.0 * np.pi / side)), np.sin(t * (2.0 * np.pi / side))], axis=2).astype(np.float32)
        for t in (row, col)
    ]


def flip_constants(side):
    lanes = np.zeros((side, side), np.float32)
    lanes[(-np.arange(side)) % side, np.arange(side)] = 1.0
    fold = np.zeros((HALF, side), np.float32)
    for u in range(1, side // 2):
        fold[u, side - u] = 1.0
    unfold = np.zeros((side // 2, HALF + 8), np.float32)
    for r in range(side // 2):
        unfold[r, side // 2 - r] = 1.0
    return lanes, fold, unfold


def scatter_kernel(class_local, chips_y, class_hbm, turn_hbm, best_hbm, bin_hbm, shift_hbm, image_ref, slot_ref,
                   class_ref, turn_ref, best_ref, bin_ref, shift_ref, count_ref, hold_ref, tag_ref,
                   int_sems, in_sems, out_sems, tag_sem):
    items, side, _ = hold_ref.shape
    pairs = ((class_hbm, class_ref), (turn_hbm, turn_ref), (best_hbm, best_ref), (bin_hbm, bin_ref), (shift_hbm, shift_ref))
    ints = [pltpu.make_async_copy(a, b, int_sems.at[at]) for at, (a, b) in enumerate(pairs)]
    for load in ints:
        load.start()
    loads = []
    for item in range(items):
        load = pltpu.make_async_copy(image_ref.at[item], hold_ref.at[item], in_sems.at[item])
        load.start()
        loads.append(load)
    for owner in range(count_ref.shape[0]):
        count_ref[owner] = 0
    tag_ref[...] = jnp.zeros_like(tag_ref)
    lane = lax.broadcasted_iota(jnp.int32, (1, side), 1)
    groups = lax.axis_size("grp")
    me_grp = lax.axis_index("grp")
    cores, own = groups // chips_y, class_local // groups
    core, me_y = lax.rem(me_grp, cores), lax.div(me_grp, cores)
    for load in ints:
        load.wait()
    stores = []
    for item in range(items):
        owner = lax.div(class_ref[item], class_local)
        local = class_ref[item] - owner * class_local
        rank = count_ref[owner]
        count_ref[owner] = rank + 1
        loads[item].wait()
        store = pltpu.make_async_copy(
            hold_ref.at[item],
            slot_ref.at[owner, pl.ds(pl.multiple_of(rank * side, side), side), 0, :],
            out_sems.at[item],
        )
        store.start()
        stores.append(store)
        place = lax.div(local, own)
        other = lax.rem(lax.rem(place, cores) - core + cores, cores)
        step = lax.rem(lax.div(place, cores) - me_y + chips_y, chips_y)
        target = (other * chips_y + step) * own + lax.rem(local, own)
        best = best_ref[item]
        fields = (local, turn_ref[item], shift_ref[0, best] + SHIFT, shift_ref[1, best] + SHIFT, bin_ref[item], target, 1)
        tag = jnp.zeros((1, side), jnp.int32)
        for at, value in enumerate(fields):
            tag = jnp.where(lane == rank * TAG + at, value, tag)
        tag_ref[owner] += tag.astype(jnp.float32)
    store = pltpu.make_async_copy(tag_ref, slot_ref.at[:, 2 * side], tag_sem)
    store.start()
    stores.append(store)
    for store in stores:
        store.wait()


def place_slots(particles, class_of, rotation_bin, shift_best, defocus_bin, shift_list, owners, class_local, chips_y):
    count, side, _ = particles.shape
    return pl.pallas_call(
        functools.partial(scatter_kernel, class_local, chips_y),
        out_shape=jax.ShapeDtypeStruct((owners, 2 * side + 1, 1, side), jnp.float32),
        in_specs=[pl.BlockSpec(memory_space=pltpu.HBM)] * 6,
        out_specs=pl.BlockSpec(memory_space=pltpu.HBM),
        scratch_shapes=[pltpu.SMEM((count,), jnp.int32)] * 4
        + [
            pltpu.SMEM(shift_list.shape[::-1], jnp.int32),
            pltpu.SMEM((owners,), jnp.int32),
            pltpu.VMEM((count, side, side), jnp.float32),
            pltpu.VMEM((owners, 1, side), jnp.float32),
            pltpu.SemaphoreType.DMA((5,)),
            pltpu.SemaphoreType.DMA((count,)),
            pltpu.SemaphoreType.DMA((count,)),
            pltpu.SemaphoreType.DMA,
        ],
        compiler_params=pltpu.CompilerParams(vmem_limit_bytes=58 * MIB),
        name="place_slots",
    )(class_of, rotation_bin, shift_best, defocus_bin, shift_list.T, particles)


def spectrum_kernel(step_sources, info_ref, image_ref, contrast_ref, turn_ref, row_ref, col_ref, left_ref, right_ref,
                    *refs):
    keep_ref, give_ref, filt_ref, numer_ref, hold_ref, sems, in_sems = refs[-7:]
    side = image_ref.shape[-1]
    first = pl.program_id(0) * step_sources

    def load(step):
        part = pl.ds(step * step_sources, step_sources)
        return pltpu.make_async_copy(
            image_ref.at[part, pl.ds(0, 2 * side), 0, :], hold_ref.at[part], in_sems.at[step]
        )

    @pl.when(pl.program_id(0) == 0)
    def _():
        load(0).start()

    lane = lax.broadcasted_iota(jnp.int32, (1, side), 1)

    @pl.when(pl.program_id(0) == 0)
    def _():
        numer_ref[...] = jnp.zeros_like(numer_ref)

    load(pl.program_id(0)).wait()

    @pl.when(pl.program_id(0) < pl.num_programs(0) - 1)
    def _():
        load(pl.program_id(0) + 1).start()

    turns = [info_ref[first + item // 2, item % 2, 1] for item in range(2 * step_sources)]
    parts = []
    for at in range(step_sources):
        highs, lows = [], []
        for k in range(2):
            image = hold_ref[first + at, k * side : (k + 1) * side]
            odd = lax.rem(turns[2 * at + k], 2) == 1
            high, low = split(jnp.where(odd, image.T, image))
            highs.append(high)
            lows.append(low)
        stacked = jnp.concatenate(
            [jnp.concatenate(highs, axis=1), jnp.concatenate(lows, axis=1)], axis=0
        )
        halfway = jnp.dot(left_ref[...], stacked, preferred_element_type=jnp.float32)
        halfway = halfway[: 2 * HALF] + halfway[2 * HALF :]
        for k in range(2):
            odd = lax.rem(turns[2 * at + k], 2) == 1
            sign = jnp.where(odd, -1.0, 1.0).astype(jnp.float32)
            lanes = slice(k * side, (k + 1) * side)
            parts.append(
                jnp.concatenate([halfway[:HALF, lanes], sign * halfway[HALF:, lanes]], axis=1)
            )
    high, low = split(jnp.concatenate(parts, axis=0))
    spectrum = jnp.dot(
        jnp.concatenate([high, low, high], axis=1), right_ref[...], preferred_element_type=jnp.float32
    )
    for item in range(2 * step_sources):
        info = [info_ref[first + item // 2, item % 2, at] for at in range(7)]
        rows = slice(item * HALF, (item + 1) * HALF)
        sign = jnp.where(turns[item] >= 2, -1.0, 1.0).astype(jnp.float32)
        real = spectrum[rows, :side]
        imag = sign * spectrum[rows, side:]
        turn = turn_ref[turns[item]]
        contrast = contrast_ref[info[4]]
        turn_real, turn_imag = turn[:, :side], turn[:, side:]
        filt_real = contrast * (real * turn_real - imag * turn_imag)
        filt_imag = contrast * (real * turn_imag + imag * turn_real)
        filt_ref[item, :, :side] = filt_real
        filt_ref[item, :, side:] = filt_imag

        @pl.when(info[6] > 0)
        def _(info=info, filt_real=filt_real, filt_imag=filt_imag):
            target = info[5]
            row_real, row_imag = row_ref[info[2], :, :side], row_ref[info[2], :, side:]
            half_real = filt_real * row_real - filt_imag * row_imag
            half_imag = filt_real * row_imag + filt_imag * row_real
            col_real, col_imag = col_ref[info[3], :, :side], col_ref[info[3], :, side:]
            numer_ref[target, :, :side] += half_real * col_real - half_imag * col_imag
            numer_ref[target, :, side:] += half_real * col_imag + half_imag * col_real
            hit = (lane == info[4]).astype(jnp.float32)
            numer_ref[target, COUNT : COUNT + 1, :side] += hit

    @pl.when(pl.program_id(0) == pl.num_programs(0) - 1)
    def _():
        half = numer_ref.shape[0] // 2
        copies = [
            pltpu.make_async_copy(numer_ref.at[pl.ds(half, half)], give_ref, sems.at[0]),
            pltpu.make_async_copy(numer_ref.at[pl.ds(0, half)], keep_ref, sems.at[1]),
        ]
        for copy in copies:
            copy.start()
        for copy in copies:
            copy.wait()


def score_kernel(step_sources, info_ref, filt_ref, ref_ref, col_ref, row_ref, score_ref):
    side = score_ref.shape[-1]
    first = pl.program_id(0) * step_sources
    products = []
    for item in range(2 * step_sources):
        ref = ref_ref[info_ref[first + item // 2, item % 2, 0]]
        ref_real, ref_imag = ref[:, :side], ref[:, side:]
        filt_real, filt_imag = filt_ref[item, :, :side], filt_ref[item, :, side:]
        products.append(
            jnp.concatenate(
                [
                    filt_real * ref_real + filt_imag * ref_imag,
                    filt_imag * ref_real - filt_real * ref_imag,
                ],
                axis=1,
            )
        )
    high, low = split(jnp.concatenate(products, axis=0))
    by_col = jnp.dot(
        jnp.concatenate([high, low], axis=1), col_ref[...], preferred_element_type=jnp.float32
    )
    by_col = by_col[:, :side] + by_col[:, side:]
    lane = lax.broadcasted_iota(jnp.int32, (1, side), 1)
    for at in range(step_sources):
        sums = []
        for k in range(2):
            item = 2 * at + k
            total = jnp.sum(
                by_col[item * HALF : (item + 1) * HALF] * row_ref[...], axis=0, keepdims=True
            )
            sums.append(total + pltpu.roll(total, side // 2, axis=1))
        score_ref[at] = jnp.where(lane < side // 2, sums[0], sums[1])


def owner_spectra(info, images, contrast, turn, row, col, left, right, ready, class_local):
    sources, _, _, side = images.shape
    step_sources = 8
    whole = lambda x: pl.BlockSpec(x.shape, lambda i: (0,) * x.ndim)
    tables = (contrast, turn, row, col, left, right)
    half = jax.ShapeDtypeStruct((class_local // 2, HALF, 2 * side), jnp.float32)
    return pl.pallas_call(
        functools.partial(spectrum_kernel, step_sources),
        grid=(sources // step_sources,),
        out_shape=(
            half,
            half,
            jax.ShapeDtypeStruct((2 * sources, HALF, 2 * side), jnp.float32),
        ),
        in_specs=[
            pl.BlockSpec(memory_space=pltpu.SMEM),
            pl.BlockSpec(memory_space=pltpu.HBM),
        ]
        + [whole(table) for table in tables]
        + [pl.BlockSpec(memory_space=pl.ANY)] * len(ready),
        out_specs=(
            pl.BlockSpec(memory_space=pltpu.HBM),
            pl.BlockSpec(memory_space=pltpu.HBM),
            pl.BlockSpec((2 * step_sources, HALF, 2 * side), lambda i: (i, 0, 0)),
        ),
        scratch_shapes=[
            pltpu.VMEM((class_local, HALF, 2 * side), jnp.float32),
            pltpu.VMEM((sources, 2 * side, side), jnp.float32),
            pltpu.SemaphoreType.DMA((2,)),
            pltpu.SemaphoreType.DMA((sources // step_sources,)),
        ],
        compiler_params=pltpu.CompilerParams(vmem_limit_bytes=32 * MIB),
        name="owner_spectra",
    )(info, images, *tables, *ready)


def owner_scores(info, filtered, refs, col, row):
    items, _, wide = filtered.shape
    step_sources = 16
    whole = lambda x: pl.BlockSpec(x.shape, lambda i: (0,) * x.ndim)
    return pl.pallas_call(
        functools.partial(score_kernel, step_sources),
        grid=(items // 2 // step_sources,),
        out_shape=jax.ShapeDtypeStruct((items // 2, 1, wide // 2), jnp.float32),
        in_specs=[
            pl.BlockSpec(memory_space=pltpu.SMEM),
            pl.BlockSpec((2 * step_sources, HALF, wide), lambda i: (i, 0, 0)),
            whole(refs), whole(col), whole(row),
        ],
        out_specs=pl.BlockSpec((step_sources, 1, wide // 2), lambda i: (i, 0, 0)),
        compiler_params=pltpu.CompilerParams(vmem_limit_bytes=40 * MIB),
        name="owner_scores",
    )(info, filtered, refs, col, row)


def finish_kernel(target_ref, mine_ref, a_ref, b_ref, c_ref, contrast_ref, lanes_ref, unfold_ref, home_ref,
                  fresh_ref, score_ref):
    classes, _, _, side = fresh_ref.shape
    squares = [contrast_ref[which] * contrast_ref[which] for which in range(contrast_ref.shape[0])]
    ratios = []
    for at in range(classes):
        total = (mine_ref[at] + a_ref[at]) + (b_ref[at] + c_ref[at])
        weight = jnp.zeros((HALF, side), jnp.float32)
        for which, square in enumerate(squares):
            weight += total[COUNT : COUNT + 1, which : which + 1] * square
        inverse = 1.0 / (weight + 1.0)
        for part in range(2):
            ratio = total[:, part * side : (part + 1) * side] * inverse
            fresh_ref[at, part, : side // 2] = ratio[: side // 2]
            ratios.append(ratio)
    high, low = split(jnp.concatenate(ratios, axis=0))
    flipped = jnp.dot(high, lanes_ref[...], preferred_element_type=jnp.float32) + jnp.dot(
        low, lanes_ref[...], preferred_element_type=jnp.float32
    )
    flipped = [flipped[at * HALF : (at + 1) * HALF] for at in range(2 * classes)]
    pad = jnp.zeros((unfold_ref.shape[1] - HALF, 2 * classes * side), jnp.float32)
    high, low = split(jnp.concatenate([jnp.concatenate(flipped, axis=1), pad], axis=0))
    back = jnp.dot(unfold_ref[...], high, preferred_element_type=jnp.float32) + jnp.dot(
        unfold_ref[...], low, preferred_element_type=jnp.float32
    )
    for at in range(classes):
        for part in range(2):
            first = (2 * at + part) * side
            block = back[:, first : first + side]
            fresh_ref[at, part, side // 2 :] = block if part == 0 else -block
    items, shifts = score_ref.shape
    for item in range(items):
        target = target_ref[item]
        row = home_ref[lax.div(target, 2)]
        row = jnp.where(lax.rem(target, 2) == 1, pltpu.roll(row, shifts, axis=1), row)
        score_ref[item : item + 1, :] = row[:, :shifts]


def finish(target, blocks, contrast, lanes, unfold, home, side):
    return pl.pallas_call(
        finish_kernel,
        out_shape=(
            jax.ShapeDtypeStruct((blocks[0].shape[0], 2, side, side), jnp.float32),
            jax.ShapeDtypeStruct((target.shape[0], side // 2), jnp.float32),
        ),
        in_specs=[pl.BlockSpec(memory_space=pltpu.SMEM)] + [pl.BlockSpec(memory_space=pltpu.VMEM)] * 8,
        compiler_params=pltpu.CompilerParams(vmem_limit_bytes=16 * MIB),
        name="finish",
    )(target, *blocks, contrast, lanes, unfold, home)


def body(
    particles, references, class_of, rotation_bin, shift_best, defocus_bin, shift_list,
    defocus, chips_y,
):
    side = particles.shape[-1]
    class_local = references.shape[0]
    owners = lax.axis_size("cls")
    groups = lax.axis_size("grp")
    unit = 2.0 * math.pi / side

    cores = groups // chips_y
    own_classes = class_local // groups

    send = place_slots(
        particles, class_of, rotation_bin, shift_best, defocus_bin, shift_list, owners, class_local, chips_y
    )
    images = lax.all_to_all(send, "cls", split_axis=0, concat_axis=0, tiled=True)

    pixel = jnp.arange(side, dtype=jnp.int32)
    signed = jnp.where(pixel < side // 2, pixel, pixel - side).astype(jnp.float32)
    half = jnp.arange(HALF, dtype=jnp.int32)
    half_signed = jnp.where(half < side // 2, half, half - side).astype(jnp.float32)
    radius = (half_signed[:, None] ** 2 + signed[None, :] ** 2) / float((side // 2) ** 2)
    angle = defocus[:, None, None] * radius[None]
    contrast = -(0.995 * jnp.sin(angle) + 0.1 * jnp.cos(angle))

    row_angle = ((half[None, :] * shift_list[:, 0][:, None]) % side).astype(jnp.float32) * unit
    col_angle = ((pixel[None, :] * shift_list[:, 1][:, None]) % side).astype(jnp.float32) * unit
    row_cos, row_sin = jnp.cos(row_angle), jnp.sin(row_angle)
    col_cos, col_sin = jnp.cos(col_angle), jnp.sin(col_angle)
    col = jnp.concatenate(
        [
            jnp.concatenate([col_cos.T, col_sin.T], axis=1),
            jnp.concatenate([-col_sin.T, col_cos.T], axis=1),
        ],
        axis=0,
    )
    col_high = lax.reduce_precision(col, exponent_bits=8, mantissa_bits=7)
    col = jnp.concatenate([col_high, col - col_high], axis=1).astype(jnp.bfloat16)
    col = jnp.concatenate([col, col], axis=0)
    row = jnp.concatenate([row_cos.T, -row_sin.T], axis=1) / side

    lanes, fold, unfold = flip_constants(side)
    live_rows = (half <= side // 2).astype(jnp.float32)[:, None]
    folded = jnp.einsum("ua,ciab->ciub", fold, references, precision=lax.Precision.HIGH)
    folded = jnp.einsum("ciub,bv->ciuv", folded, lanes, precision=lax.Precision.HIGH)
    top = references[:, :, :HALF] * live_rows
    refs = jnp.concatenate([top[:, 0] + folded[:, 0], top[:, 1] - folded[:, 1]], axis=2)

    refs = pltpu.with_memory_space_constraint(refs, pltpu.HBM)
    info = images[:, 2 * side, 0, : 2 * TAG].astype(jnp.int32).reshape(owners, 2, TAG)
    left, right = dft_constants(side)
    best_row, best_col = shift_constants(side)
    keep, give, filtered = owner_spectra(
        info, images, contrast, jnp.asarray(turn_constants(side)), jnp.asarray(best_row),
        jnp.asarray(best_col), jnp.asarray(left), jnp.asarray(right), (refs, col, row), class_local,
    )
    slot_scores = owner_scores(info, filtered, refs, col, row)

    got = lax.ppermute(give, "grp", [(i, i ^ 1) for i in range(groups)])
    got, slot_scores = lax.optimization_barrier((got, slot_scores))
    blocks = {}
    for step in (2, 1, 3, 0):
        part = slice(step * own_classes, (step + 1) * own_classes)
        block = keep[part] + got[part]
        pairs = [(i, ((i // cores + step) % chips_y) * cores + i % cores) for i in range(groups)]
        blocks[step] = lax.ppermute(block, "grp", pairs) if step else block

    home = lax.all_to_all(slot_scores, "cls", split_axis=0, concat_axis=0, tiled=True)
    owner_of = class_of // class_local
    earlier = jnp.tril(owner_of[:, None] == owner_of[None, :], -1)
    target = owner_of * 2 + jnp.sum(earlier.astype(jnp.int32), axis=1)
    fresh_refs, scores = finish(
        target, [blocks[step] for step in range(chips_y)], contrast, jnp.asarray(lanes, jnp.bfloat16),
        jnp.asarray(unfold, jnp.bfloat16), home, side,
    )
    return (scores, fresh_refs)


def solution(mesh):
    chips_y = mesh.shape["grp"] // 2
    return jax.shard_map(
        functools.partial(body, chips_y=chips_y),
        mesh=mesh,
        in_specs=(
            P(("grp", "cls"), None, None),
            P("cls", None, None, None),
            P(("grp", "cls")),
            P(("grp", "cls")),
            P(("grp", "cls")),
            P(("grp", "cls")),
            P(),
            P(),
        ),
        out_specs=(P(("grp", "cls"), None), P(("cls", "grp"), None, None, None)),
        check_vma=False,
    )
```

```python
import functools
import math

import jax
import jax.numpy as jnp
import numpy as np
from jax import lax
from jax.experimental import pallas as pl
from jax.experimental.pallas import tpu as pltpu
from jax.sharding import PartitionSpec as P

HALF = 72
TAG = 8
COUNT = HALF - 1
SHIFT = 8
MIB = 1 << 20


def split_np(table):
    high = table.astype(jnp.bfloat16)
    low = (table - high.astype(np.float32)).astype(jnp.bfloat16)
    return high, low


def split(values):
    high = values.astype(jnp.bfloat16)
    low = (values - high.astype(jnp.float32)).astype(jnp.bfloat16)
    return high, low


def dft_constants(side):
    grid = np.outer(np.arange(side), np.arange(side)) % side
    angles = grid * (2.0 * np.pi / side)
    cos_table = (np.cos(angles) / np.sqrt(side)).astype(np.float32)
    sin_table = (np.sin(angles) / np.sqrt(side)).astype(np.float32)
    rows = side // 2 + 1
    left = np.zeros((2, HALF, side), np.float32)
    left[0, :rows] = cos_table[:rows]
    left[1, :rows] = sin_table[:rows]
    left_high, left_low = split_np(left.reshape(2 * HALF, side))
    left_table = np.concatenate(
        [
            np.concatenate([left_high, left_high], axis=1),
            np.concatenate([left_low, np.zeros_like(left_low)], axis=1),
        ],
        axis=0,
    )
    right = np.block([[cos_table, -sin_table], [-sin_table, -cos_table]]).astype(np.float32)
    right_high, right_low = split_np(right)
    return left_table, np.concatenate([right_high, right_high, right_low], axis=0)


def turn_constants(side):
    row = np.arange(HALF)[:, None] + 0 * np.arange(side)[None, :]
    col = 0 * np.arange(HALF)[:, None] + np.arange(side)[None, :]
    shifts = np.stack([0 * row, row, row + col, col]) % side
    angles = shifts * (2.0 * np.pi / side)
    return np.concatenate([np.cos(angles), np.sin(angles)], axis=2).astype(np.float32)


def shift_constants(side):
    steps = np.arange(-SHIFT, SHIFT + 1)[:, None]
    row = np.broadcast_to((steps * np.arange(HALF) % side)[:, :, None], (2 * SHIFT + 1, HALF, side))
    col = (steps * np.arange(side) % side)[:, None, :]
    return [
        np.concatenate([np.cos(t * (2.0 * np.pi / side)), np.sin(t * (2.0 * np.pi / side))], axis=2).astype(np.float32)
        for t in (row, col)
    ]


def flip_constants(side):
    lanes = np.zeros((side, side), np.float32)
    lanes[(-np.arange(side)) % side, np.arange(side)] = 1.0
    fold = np.zeros((HALF, side), np.float32)
    for u in range(1, side // 2):
        fold[u, side - u] = 1.0
    unfold = np.zeros((side // 2, HALF + 8), np.float32)
    for r in range(side // 2):
        unfold[r, side // 2 - r] = 1.0
    return lanes, fold, unfold


def scatter_kernel(class_local, chips_y, class_hbm, turn_hbm, best_hbm, bin_hbm, shift_hbm, image_ref, slot_ref,
                   class_ref, turn_ref, best_ref, bin_ref, shift_ref, count_ref, hold_ref, tag_ref,
                   int_sems, in_sems, out_sems, tag_sem):
    items, side, _ = hold_ref.shape
    pairs = ((class_hbm, class_ref), (turn_hbm, turn_ref), (best_hbm, best_ref), (bin_hbm, bin_ref), (shift_hbm, shift_ref))
    ints = [pltpu.make_async_copy(a, b, int_sems.at[at]) for at, (a, b) in enumerate(pairs)]
    for load in ints:
        load.start()
    loads = []
    for item in range(items):
        load = pltpu.make_async_copy(image_ref.at[item], hold_ref.at[item], in_sems.at[item])
        load.start()
        loads.append(load)
    for owner in range(count_ref.shape[0]):
        count_ref[owner] = 0
    tag_ref[...] = jnp.zeros_like(tag_ref)
    lane = lax.broadcasted_iota(jnp.int32, (1, side), 1)
    groups = lax.axis_size("grp")
    me_grp = lax.axis_index("grp")
    cores, own = groups // chips_y, class_local // groups
    core, me_y = lax.rem(me_grp, cores), lax.div(me_grp, cores)
    for load in ints:
        load.wait()
    stores = []
    for item in range(items):
        owner = lax.div(class_ref[item], class_local)
        rank = count_ref[owner]
        count_ref[owner] = rank + 1
        loads[item].wait()
        store = pltpu.make_async_copy(
            hold_ref.at[item],
            slot_ref.at[owner, pl.ds(pl.multiple_of(rank * side, side), side), 0, :],
            out_sems.at[item],
        )
        store.start()
        stores.append(store)
        local = class_ref[item] - owner * class_local
        place = lax.div(local, own)
        other = lax.rem(lax.rem(place, cores) - core + cores, cores)
        step = lax.rem(lax.div(place, cores) - me_y + chips_y, chips_y)
        target = (other * chips_y + step) * own + lax.rem(local, own)
        best = best_ref[item]
        fields = (local, turn_ref[item], shift_ref[0, best] + SHIFT, shift_ref[1, best] + SHIFT, bin_ref[item], target, 1)
        tag = jnp.zeros((1, side), jnp.int32)
        for at, value in enumerate(fields):
            tag = jnp.where(lane == rank * TAG + at, value, tag)
        tag_ref[owner] += tag.astype(jnp.float32)
    store = pltpu.make_async_copy(tag_ref, slot_ref.at[:, 2 * side], tag_sem)
    store.start()
    stores.append(store)
    for store in stores:
        store.wait()


def place_slots(particles, class_of, rotation_bin, shift_best, defocus_bin, shift_list, owners, class_local, chips_y):
    count, side, _ = particles.shape
    return pl.pallas_call(
        functools.partial(scatter_kernel, class_local, chips_y),
        out_shape=jax.ShapeDtypeStruct((owners, 2 * side + 1, 1, side), jnp.float32),
        in_specs=[pl.BlockSpec(memory_space=pltpu.HBM)] * 6,
        out_specs=pl.BlockSpec(memory_space=pltpu.HBM),
        scratch_shapes=[pltpu.SMEM((count,), jnp.int32)] * 4
        + [
            pltpu.SMEM(shift_list.shape[::-1], jnp.int32),
            pltpu.SMEM((owners,), jnp.int32),
            pltpu.VMEM((count, side, side), jnp.float32),
            pltpu.VMEM((owners, 1, side), jnp.float32),
            pltpu.SemaphoreType.DMA((5,)),
            pltpu.SemaphoreType.DMA((count,)),
            pltpu.SemaphoreType.DMA((count,)),
            pltpu.SemaphoreType.DMA,
        ],
        compiler_params=pltpu.CompilerParams(vmem_limit_bytes=58 * MIB),
        name="place_slots",
    )(class_of, rotation_bin, shift_best, defocus_bin, shift_list.T, particles)


def read_tag(tag_ref, source, slot, at):
    return tag_ref[source, 0, slot * TAG + at].astype(jnp.int32)


def spectrum_kernel(step_sources, image_ref, contrast_ref, turn_ref, row_ref, col_ref, left_ref, right_ref,
                    *refs):
    keep_ref, give_ref, filt_ref, local_ref, numer_ref, hold_ref, tag_ref, sems, in_sems, tag_sem = refs[-10:]
    side = image_ref.shape[-1]
    first = pl.program_id(0) * step_sources
    lane = lax.broadcasted_iota(jnp.int32, (1, side), 1)

    def load(step):
        part = pl.ds(step * step_sources, step_sources)
        return pltpu.make_async_copy(
            image_ref.at[part, pl.ds(0, 2 * side), 0, :], hold_ref.at[part], in_sems.at[step]
        )

    @pl.when(pl.program_id(0) == 0)
    def _():
        tags = pltpu.make_async_copy(image_ref.at[:, 2 * side], tag_ref, tag_sem)
        tags.start()
        load(0).start()
        numer_ref[...] = jnp.zeros_like(numer_ref)
        tags.wait()

    load(pl.program_id(0)).wait()

    @pl.when(pl.program_id(0) < pl.num_programs(0) - 1)
    def _():
        load(pl.program_id(0) + 1).start()

    turns = [read_tag(tag_ref, first + item // 2, item % 2, 1) for item in range(2 * step_sources)]
    parts = []
    for at in range(step_sources):
        highs, lows = [], []
        for k in range(2):
            image = hold_ref[first + at, k * side : (k + 1) * side]
            odd = lax.rem(turns[2 * at + k], 2) == 1
            high, low = split(jnp.where(odd, image.T, image))
            highs.append(high)
            lows.append(low)
        stacked = jnp.concatenate(
            [jnp.concatenate(highs, axis=1), jnp.concatenate(lows, axis=1)], axis=0
        )
        halfway = jnp.dot(left_ref[...], stacked, preferred_element_type=jnp.float32)
        halfway = halfway[: 2 * HALF] + halfway[2 * HALF :]
        for k in range(2):
            odd = lax.rem(turns[2 * at + k], 2) == 1
            sign = jnp.where(odd, -1.0, 1.0).astype(jnp.float32)
            lanes = slice(k * side, (k + 1) * side)
            parts.append(
                jnp.concatenate([halfway[:HALF, lanes], sign * halfway[HALF:, lanes]], axis=1)
            )
    high, low = split(jnp.concatenate(parts, axis=0))
    spectrum = jnp.dot(
        jnp.concatenate([high, low, high], axis=1), right_ref[...], preferred_element_type=jnp.float32
    )
    for item in range(2 * step_sources):
        info = [read_tag(tag_ref, first + item // 2, item % 2, at) for at in range(7)]
        local_ref[2 * first + item] = info[0]
        rows = slice(item * HALF, (item + 1) * HALF)
        sign = jnp.where(turns[item] >= 2, -1.0, 1.0).astype(jnp.float32)
        real = spectrum[rows, :side]
        imag = sign * spectrum[rows, side:]
        turn = turn_ref[turns[item]]
        contrast = contrast_ref[info[4]]
        turn_real, turn_imag = turn[:, :side], turn[:, side:]
        filt_real = contrast * (real * turn_real - imag * turn_imag)
        filt_imag = contrast * (real * turn_imag + imag * turn_real)
        filt_ref[item, :, :side] = filt_real
        filt_ref[item, :, side:] = filt_imag

        @pl.when(info[6] > 0)
        def _(info=info, filt_real=filt_real, filt_imag=filt_imag):
            target = info[5]
            row_real, row_imag = row_ref[info[2], :, :side], row_ref[info[2], :, side:]
            half_real = filt_real * row_real - filt_imag * row_imag
            half_imag = filt_real * row_imag + filt_imag * row_real
            col_real, col_imag = col_ref[info[3], :, :side], col_ref[info[3], :, side:]
            numer_ref[target, :, :side] += half_real * col_real - half_imag * col_imag
            numer_ref[target, :, side:] += half_real * col_imag + half_imag * col_real
            hit = (lane == info[4]).astype(jnp.float32)
            numer_ref[target, COUNT : COUNT + 1, :side] += hit

    @pl.when(pl.program_id(0) == pl.num_programs(0) - 1)
    def _():
        half = numer_ref.shape[0] // 2
        copies = [
            pltpu.make_async_copy(numer_ref.at[pl.ds(half, half)], give_ref, sems.at[0]),
            pltpu.make_async_copy(numer_ref.at[pl.ds(0, half)], keep_ref, sems.at[1]),
        ]
        for copy in copies:
            copy.start()
        for copy in copies:
            copy.wait()


def score_kernel(step_sources, local_ref, filt_ref, ref_ref, col_ref, row_ref, score_ref):
    side = score_ref.shape[-1]
    first = pl.program_id(0) * step_sources * 2
    products = []
    for item in range(2 * step_sources):
        ref = ref_ref[local_ref[first + item]]
        ref_real, ref_imag = ref[:, :side], ref[:, side:]
        filt_real, filt_imag = filt_ref[item, :, :side], filt_ref[item, :, side:]
        products.append(
            jnp.concatenate(
                [
                    filt_real * ref_real + filt_imag * ref_imag,
                    filt_imag * ref_real - filt_real * ref_imag,
                ],
                axis=1,
            )
        )
    high, low = split(jnp.concatenate(products, axis=0))
    by_col = jnp.dot(
        jnp.concatenate([high, low], axis=1), col_ref[...], preferred_element_type=jnp.float32
    )
    by_col = by_col[:, :side] + by_col[:, side:]
    lane = lax.broadcasted_iota(jnp.int32, (1, side), 1)
    for at in range(step_sources):
        sums = []
        for k in range(2):
            item = 2 * at + k
            total = jnp.sum(
                by_col[item * HALF : (item + 1) * HALF] * row_ref[...], axis=0, keepdims=True
            )
            sums.append(total + pltpu.roll(total, side // 2, axis=1))
        score_ref[at] = jnp.where(lane < side // 2, sums[0], sums[1])


def owner_spectra(images, contrast, turn, row, col, left, right, ready, class_local):
    sources, _, _, side = images.shape
    step_sources = 8
    whole = lambda x: pl.BlockSpec(x.shape, lambda i: (0,) * x.ndim)
    tables = (contrast, turn, row, col, left, right)
    half = jax.ShapeDtypeStruct((class_local // 2, HALF, 2 * side), jnp.float32)
    return pl.pallas_call(
        functools.partial(spectrum_kernel, step_sources),
        grid=(sources // step_sources,),
        out_shape=(
            half,
            half,
            jax.ShapeDtypeStruct((2 * sources, HALF, 2 * side), jnp.float32),
            jax.ShapeDtypeStruct((2 * sources,), jnp.int32),
        ),
        in_specs=[pl.BlockSpec(memory_space=pltpu.HBM)]
        + [whole(table) for table in tables]
        + [pl.BlockSpec(memory_space=pl.ANY)] * len(ready),
        out_specs=(
            pl.BlockSpec(memory_space=pltpu.HBM),
            pl.BlockSpec(memory_space=pltpu.HBM),
            pl.BlockSpec((2 * step_sources, HALF, 2 * side), lambda i: (i, 0, 0)),
            pl.BlockSpec(memory_space=pltpu.SMEM),
        ),
        scratch_shapes=[
            pltpu.VMEM((class_local, HALF, 2 * side), jnp.float32),
            pltpu.VMEM((sources, 2 * side, side), jnp.float32),
            pltpu.SMEM((sources, 1, side), jnp.float32),
            pltpu.SemaphoreType.DMA((2,)),
            pltpu.SemaphoreType.DMA((sources // step_sources,)),
            pltpu.SemaphoreType.DMA,
        ],
        compiler_params=pltpu.CompilerParams(vmem_limit_bytes=32 * MIB),
        name="owner_spectra",
    )(images, *tables, *ready)


def owner_scores(local, filtered, refs, col, row):
    items, _, wide = filtered.shape
    step_sources = 16
    whole = lambda x: pl.BlockSpec(x.shape, lambda i: (0,) * x.ndim)
    return pl.pallas_call(
        functools.partial(score_kernel, step_sources),
        grid=(items // 2 // step_sources,),
        out_shape=jax.ShapeDtypeStruct((items // 2, 1, wide // 2), jnp.float32),
        in_specs=[
            pl.BlockSpec(memory_space=pltpu.SMEM),
            pl.BlockSpec((2 * step_sources, HALF, wide), lambda i: (i, 0, 0)),
            whole(refs), whole(col), whole(row),
        ],
        out_specs=pl.BlockSpec((step_sources, 1, wide // 2), lambda i: (i, 0, 0)),
        compiler_params=pltpu.CompilerParams(vmem_limit_bytes=40 * MIB),
        name="owner_scores",
    )(local, filtered, refs, col, row)


def finish_kernel(target_ref, mine_ref, a_ref, b_ref, c_ref, contrast_ref, lanes_ref, unfold_ref, home_ref,
                  fresh_ref, score_ref):
    classes, _, _, side = fresh_ref.shape
    squares = [contrast_ref[which] * contrast_ref[which] for which in range(contrast_ref.shape[0])]
    ratios = []
    for at in range(classes):
        total = (mine_ref[at] + a_ref[at]) + (b_ref[at] + c_ref[at])
        weight = jnp.zeros((HALF, side), jnp.float32)
        for which, square in enumerate(squares):
            weight += total[COUNT : COUNT + 1, which : which + 1] * square
        inverse = 1.0 / (weight + 1.0)
        for part in range(2):
            ratio = total[:, part * side : (part + 1) * side] * inverse
            fresh_ref[at, part, : side // 2] = ratio[: side // 2]
            ratios.append(ratio)
    high, low = split(jnp.concatenate(ratios, axis=0))
    flipped = jnp.dot(high, lanes_ref[...], preferred_element_type=jnp.float32) + jnp.dot(
        low, lanes_ref[...], preferred_element_type=jnp.float32
    )
    flipped = [flipped[at * HALF : (at + 1) * HALF] for at in range(2 * classes)]
    pad = jnp.zeros((unfold_ref.shape[1] - HALF, 2 * classes * side), jnp.float32)
    high, low = split(jnp.concatenate([jnp.concatenate(flipped, axis=1), pad], axis=0))
    back = jnp.dot(unfold_ref[...], high, preferred_element_type=jnp.float32) + jnp.dot(
        unfold_ref[...], low, preferred_element_type=jnp.float32
    )
    for at in range(classes):
        for part in range(2):
            first = (2 * at + part) * side
            block = back[:, first : first + side]
            fresh_ref[at, part, side // 2 :] = block if part == 0 else -block
    items, shifts = score_ref.shape
    for item in range(items):
        target = target_ref[item]
        row = home_ref[lax.div(target, 2)]
        row = jnp.where(lax.rem(target, 2) == 1, pltpu.roll(row, shifts, axis=1), row)
        score_ref[item : item + 1, :] = row[:, :shifts]


def finish(target, blocks, contrast, lanes, unfold, home, side):
    return pl.pallas_call(
        finish_kernel,
        out_shape=(
            jax.ShapeDtypeStruct((blocks[0].shape[0], 2, side, side), jnp.float32),
            jax.ShapeDtypeStruct((target.shape[0], side // 2), jnp.float32),
        ),
        in_specs=[pl.BlockSpec(memory_space=pltpu.SMEM)] + [pl.BlockSpec(memory_space=pltpu.VMEM)] * 8,
        compiler_params=pltpu.CompilerParams(vmem_limit_bytes=16 * MIB),
        name="finish",
    )(target, *blocks, contrast, lanes, unfold, home)


def body(
    particles, references, class_of, rotation_bin, shift_best, defocus_bin, shift_list,
    defocus, chips_y,
):
    side = particles.shape[-1]
    class_local = references.shape[0]
    owners = lax.axis_size("cls")
    groups = lax.axis_size("grp")
    unit = 2.0 * math.pi / side

    cores = groups // chips_y
    own_classes = class_local // groups

    send = place_slots(
        particles, class_of, rotation_bin, shift_best, defocus_bin, shift_list, owners, class_local, chips_y
    )
    images = lax.all_to_all(send, "cls", split_axis=0, concat_axis=0, tiled=True)

    pixel = jnp.arange(side, dtype=jnp.int32)
    signed = jnp.where(pixel < side // 2, pixel, pixel - side).astype(jnp.float32)
    half = jnp.arange(HALF, dtype=jnp.int32)
    half_signed = jnp.where(half < side // 2, half, half - side).astype(jnp.float32)
    radius = (half_signed[:, None] ** 2 + signed[None, :] ** 2) / float((side // 2) ** 2)
    angle = defocus[:, None, None] * radius[None]
    contrast = -(0.995 * jnp.sin(angle) + 0.1 * jnp.cos(angle))

    row_angle = ((half[None, :] * shift_list[:, 0][:, None]) % side).astype(jnp.float32) * unit
    col_angle = ((pixel[None, :] * shift_list[:, 1][:, None]) % side).astype(jnp.float32) * unit
    row_cos, row_sin = jnp.cos(row_angle), jnp.sin(row_angle)
    col_cos, col_sin = jnp.cos(col_angle), jnp.sin(col_angle)
    col = jnp.concatenate(
        [
            jnp.concatenate([col_cos.T, col_sin.T], axis=1),
            jnp.concatenate([-col_sin.T, col_cos.T], axis=1),
        ],
        axis=0,
    )
    col_high = lax.reduce_precision(col, exponent_bits=8, mantissa_bits=7)
    col = jnp.concatenate([col_high, col - col_high], axis=1).astype(jnp.bfloat16)
    col = jnp.concatenate([col, col], axis=0)
    row = jnp.concatenate([row_cos.T, -row_sin.T], axis=1) / side

    lanes, fold, unfold = flip_constants(side)
    live_rows = (half <= side // 2).astype(jnp.float32)[:, None]
    folded = jnp.einsum("ua,ciab->ciub", fold, references, precision=lax.Precision.HIGH)
    folded = jnp.einsum("ciub,bv->ciuv", folded, lanes, precision=lax.Precision.HIGH)
    top = references[:, :, :HALF] * live_rows
    refs = jnp.concatenate([top[:, 0] + folded[:, 0], top[:, 1] - folded[:, 1]], axis=2)

    refs = pltpu.with_memory_space_constraint(refs, pltpu.HBM)
    left, right = dft_constants(side)
    best_row, best_col = shift_constants(side)
    keep, give, filtered, local = owner_spectra(
        images, contrast, jnp.asarray(turn_constants(side)), jnp.asarray(best_row),
        jnp.asarray(best_col), jnp.asarray(left), jnp.asarray(right), (refs, col, row), class_local,
    )
    slot_scores = owner_scores(local, filtered, refs, col, row)

    got = lax.ppermute(give, "grp", [(i, i ^ 1) for i in range(groups)])
    got, slot_scores = lax.optimization_barrier((got, slot_scores))
    blocks = {}
    for step in (2, 1, 3, 0):
        part = slice(step * own_classes, (step + 1) * own_classes)
        block = keep[part] + got[part]
        pairs = [(i, ((i // cores + step) % chips_y) * cores + i % cores) for i in range(groups)]
        blocks[step] = lax.ppermute(block, "grp", pairs) if step else block

    home = lax.all_to_all(slot_scores, "cls", split_axis=0, concat_axis=0, tiled=True)
    owner_of = class_of // class_local
    earlier = jnp.tril(owner_of[:, None] == owner_of[None, :], -1)
    target = owner_of * 2 + jnp.sum(earlier.astype(jnp.int32), axis=1)
    fresh_refs, scores = finish(
        target, [blocks[step] for step in range(chips_y)], contrast, jnp.asarray(lanes, jnp.bfloat16),
        jnp.asarray(unfold, jnp.bfloat16), home, side,
    )
    return (scores, fresh_refs)


def solution(mesh):
    chips_y = mesh.shape["grp"] // 2
    return jax.shard_map(
        functools.partial(body, chips_y=chips_y),
        mesh=mesh,
        in_specs=(
            P(("grp", "cls"), None, None),
            P("cls", None, None, None),
            P(("grp", "cls")),
            P(("grp", "cls")),
            P(("grp", "cls")),
            P(("grp", "cls")),
            P(),
            P(),
        ),
        out_specs=(P(("grp", "cls"), None), P(("cls", "grp"), None, None, None)),
        check_vma=False,
    )
```

```python
import functools
import math

import jax
import jax.numpy as jnp
import numpy as np
from jax import lax
from jax.experimental import pallas as pl
from jax.experimental.pallas import tpu as pltpu
from jax.sharding import PartitionSpec as P

HALF = 72
TAG = 8
COUNT = HALF - 1
SHIFT = 8
MIB = 1 << 20


def split_np(table):
    high = table.astype(jnp.bfloat16)
    low = (table - high.astype(np.float32)).astype(jnp.bfloat16)
    return high, low


def split(values):
    high = values.astype(jnp.bfloat16)
    low = (values - high.astype(jnp.float32)).astype(jnp.bfloat16)
    return high, low


def dft_constants(side):
    grid = np.outer(np.arange(side), np.arange(side)) % side
    angles = grid * (2.0 * np.pi / side)
    cos_table = (np.cos(angles) / np.sqrt(side)).astype(np.float32)
    sin_table = (np.sin(angles) / np.sqrt(side)).astype(np.float32)
    rows = side // 2 + 1
    left = np.zeros((2, HALF, side), np.float32)
    left[0, :rows] = cos_table[:rows]
    left[1, :rows] = sin_table[:rows]
    left_high, left_low = split_np(left.reshape(2 * HALF, side))
    left_table = np.concatenate(
        [
            np.concatenate([left_high, left_high], axis=1),
            np.concatenate([left_low, np.zeros_like(left_low)], axis=1),
        ],
        axis=0,
    )
    right = np.block([[cos_table, -sin_table], [-sin_table, -cos_table]]).astype(np.float32)
    right_high, right_low = split_np(right)
    return left_table, np.concatenate([right_high, right_high, right_low], axis=0)


def turn_constants(side):
    row = np.arange(HALF)[:, None] + 0 * np.arange(side)[None, :]
    col = 0 * np.arange(HALF)[:, None] + np.arange(side)[None, :]
    shifts = np.stack([0 * row, row, row + col, col]) % side
    angles = shifts * (2.0 * np.pi / side)
    return np.concatenate([np.cos(angles), np.sin(angles)], axis=2).astype(np.float32)


def shift_constants(side):
    steps = np.arange(-SHIFT, SHIFT + 1)[:, None]
    row = np.broadcast_to((steps * np.arange(HALF) % side)[:, :, None], (2 * SHIFT + 1, HALF, side))
    col = (steps * np.arange(side) % side)[:, None, :]
    return [
        np.concatenate([np.cos(t * (2.0 * np.pi / side)), np.sin(t * (2.0 * np.pi / side))], axis=2).astype(np.float32)
        for t in (row, col)
    ]


def flip_constants(side):
    lanes = np.zeros((side, side), np.float32)
    lanes[(-np.arange(side)) % side, np.arange(side)] = 1.0
    fold = np.zeros((HALF, side), np.float32)
    for u in range(1, side // 2):
        fold[u, side - u] = 1.0
    unfold = np.zeros((side // 2, HALF + 8), np.float32)
    for r in range(side // 2):
        unfold[r, side // 2 - r] = 1.0
    return lanes, fold, unfold


def scatter_kernel(class_local, chips_y, class_hbm, turn_hbm, best_hbm, bin_hbm, shift_hbm, image_ref, slot_ref,
                   class_ref, turn_ref, best_ref, bin_ref, shift_ref, count_ref, hold_ref, tag_ref,
                   int_sems, in_sems, out_sems, tag_sem):
    items, side, _ = hold_ref.shape
    pairs = ((class_hbm, class_ref), (turn_hbm, turn_ref), (best_hbm, best_ref), (bin_hbm, bin_ref), (shift_hbm, shift_ref))
    ints = [pltpu.make_async_copy(a, b, int_sems.at[at]) for at, (a, b) in enumerate(pairs)]
    for load in ints:
        load.start()
    loads = []
    for item in range(items):
        load = pltpu.make_async_copy(image_ref.at[item], hold_ref.at[item], in_sems.at[item])
        load.start()
        loads.append(load)
    for owner in range(count_ref.shape[0]):
        count_ref[owner] = 0
    tag_ref[...] = jnp.zeros_like(tag_ref)
    lane = lax.broadcasted_iota(jnp.int32, (1, side), 1)
    groups = lax.axis_size("grp")
    me_grp = lax.axis_index("grp")
    cores, own = groups // chips_y, class_local // groups
    core, me_y = lax.rem(me_grp, cores), lax.div(me_grp, cores)
    for load in ints:
        load.wait()
    stores = []
    for item in range(items):
        owner = lax.div(class_ref[item], class_local)
        rank = count_ref[owner]
        count_ref[owner] = rank + 1
        loads[item].wait()
        store = pltpu.make_async_copy(
            hold_ref.at[item],
            slot_ref.at[owner, pl.ds(pl.multiple_of(rank * side, side), side), 0, :],
            out_sems.at[item],
        )
        store.start()
        stores.append(store)
        local = class_ref[item] - owner * class_local
        place = lax.div(local, own)
        other = lax.rem(lax.rem(place, cores) - core + cores, cores)
        step = lax.rem(lax.div(place, cores) - me_y + chips_y, chips_y)
        target = (other * chips_y + step) * own + lax.rem(local, own)
        best = best_ref[item]
        fields = (local, turn_ref[item], shift_ref[0, best] + SHIFT, shift_ref[1, best] + SHIFT, bin_ref[item], target, 1)
        tag = jnp.zeros((1, side), jnp.int32)
        for at, value in enumerate(fields):
            tag = jnp.where(lane == rank * TAG + at, value, tag)
        tag_ref[owner] += tag.astype(jnp.float32)
    store = pltpu.make_async_copy(tag_ref, slot_ref.at[:, 2 * side], tag_sem)
    store.start()
    stores.append(store)
    for store in stores:
        store.wait()


def place_slots(particles, class_of, rotation_bin, shift_best, defocus_bin, shift_list, owners, class_local, chips_y):
    count, side, _ = particles.shape
    return pl.pallas_call(
        functools.partial(scatter_kernel, class_local, chips_y),
        out_shape=jax.ShapeDtypeStruct((owners, 2 * side + 1, 1, side), jnp.float32),
        in_specs=[pl.BlockSpec(memory_space=pltpu.HBM)] * 6,
        out_specs=pl.BlockSpec(memory_space=pltpu.HBM),
        scratch_shapes=[pltpu.SMEM((count,), jnp.int32)] * 4
        + [
            pltpu.SMEM(shift_list.shape[::-1], jnp.int32),
            pltpu.SMEM((owners,), jnp.int32),
            pltpu.VMEM((count, side, side), jnp.float32),
            pltpu.VMEM((owners, 1, side), jnp.float32),
            pltpu.SemaphoreType.DMA((5,)),
            pltpu.SemaphoreType.DMA((count,)),
            pltpu.SemaphoreType.DMA((count,)),
            pltpu.SemaphoreType.DMA,
        ],
        compiler_params=pltpu.CompilerParams(vmem_limit_bytes=58 * MIB),
        name="place_slots",
    )(class_of, rotation_bin, shift_best, defocus_bin, shift_list.T, particles)


def read_tag(tag_ref, source, slot, at):
    return tag_ref[source, 0, slot * TAG + at].astype(jnp.int32)


def spectrum_kernel(step_sources, image_ref, contrast_ref, turn_ref, row_ref, col_ref, left_ref, right_ref,
                    *refs):
    keep_ref, give_ref, filt_ref, local_ref, numer_ref, hold_ref, tag_ref, sems, in_sems, tag_sem = refs[-10:]
    side = image_ref.shape[-1]
    first = pl.program_id(0) * step_sources
    lane = lax.broadcasted_iota(jnp.int32, (1, side), 1)

    def load(step):
        part = pl.ds(step * step_sources, step_sources)
        return pltpu.make_async_copy(
            image_ref.at[part, pl.ds(0, 2 * side), 0, :], hold_ref.at[part], in_sems.at[step]
        )

    @pl.when(pl.program_id(0) == 0)
    def _():
        tags = pltpu.make_async_copy(image_ref.at[:, 2 * side], tag_ref, tag_sem)
        tags.start()
        load(0).start()
        numer_ref[...] = jnp.zeros_like(numer_ref)
        tags.wait()

    load(pl.program_id(0)).wait()

    @pl.when(pl.program_id(0) < pl.num_programs(0) - 1)
    def _():
        load(pl.program_id(0) + 1).start()

    turns = [read_tag(tag_ref, first + item // 2, item % 2, 1) for item in range(2 * step_sources)]
    parts = []
    for at in range(step_sources):
        highs, lows = [], []
        for k in range(2):
            image = hold_ref[first + at, k * side : (k + 1) * side]
            odd = lax.rem(turns[2 * at + k], 2) == 1
            high, low = split(jnp.where(odd, image.T, image))
            highs.append(high)
            lows.append(low)
        stacked = jnp.concatenate(
            [jnp.concatenate(highs, axis=1), jnp.concatenate(lows, axis=1)], axis=0
        )
        halfway = jnp.dot(left_ref[...], stacked, preferred_element_type=jnp.float32)
        halfway = halfway[: 2 * HALF] + halfway[2 * HALF :]
        for k in range(2):
            odd = lax.rem(turns[2 * at + k], 2) == 1
            sign = jnp.where(odd, -1.0, 1.0).astype(jnp.float32)
            lanes = slice(k * side, (k + 1) * side)
            parts.append(
                jnp.concatenate([halfway[:HALF, lanes], sign * halfway[HALF:, lanes]], axis=1)
            )
    high, low = split(jnp.concatenate(parts, axis=0))
    spectrum = jnp.dot(
        jnp.concatenate([high, low, high], axis=1), right_ref[...], preferred_element_type=jnp.float32
    )
    for item in range(2 * step_sources):
        info = [read_tag(tag_ref, first + item // 2, item % 2, at) for at in range(7)]
        local_ref[2 * first + item] = info[0]
        rows = slice(item * HALF, (item + 1) * HALF)
        sign = jnp.where(turns[item] >= 2, -1.0, 1.0).astype(jnp.float32)
        real = spectrum[rows, :side]
        imag = sign * spectrum[rows, side:]
        turn = turn_ref[turns[item]]
        contrast = contrast_ref[info[4]]
        turn_real, turn_imag = turn[:, :side], turn[:, side:]
        filt_real = contrast * (real * turn_real - imag * turn_imag)
        filt_imag = contrast * (real * turn_imag + imag * turn_real)
        filt_ref[item, :, :side] = filt_real
        filt_ref[item, :, side:] = filt_imag

        live = info[6] > 0
        target = info[5]
        row_real, row_imag = row_ref[info[2], :, :side], row_ref[info[2], :, side:]
        half_real = filt_real * row_real - filt_imag * row_imag
        half_imag = filt_real * row_imag + filt_imag * row_real
        col_real, col_imag = col_ref[info[3], :, :side], col_ref[info[3], :, side:]
        numer_ref[target, :, :side] += jnp.where(live, half_real * col_real - half_imag * col_imag, 0.0)
        numer_ref[target, :, side:] += jnp.where(live, half_real * col_imag + half_imag * col_real, 0.0)
        hit = ((lane == info[4]) & live).astype(jnp.float32)
        numer_ref[target, COUNT : COUNT + 1, :side] += hit

    @pl.when(pl.program_id(0) == pl.num_programs(0) - 1)
    def _():
        half = numer_ref.shape[0] // 2
        copies = [
            pltpu.make_async_copy(numer_ref.at[pl.ds(half, half)], give_ref, sems.at[0]),
            pltpu.make_async_copy(numer_ref.at[pl.ds(0, half)], keep_ref, sems.at[1]),
        ]
        for copy in copies:
            copy.start()
        for copy in copies:
            copy.wait()


def score_kernel(step_sources, local_ref, filt_ref, ref_ref, col_ref, row_ref, score_ref):
    side = score_ref.shape[-1]
    first = pl.program_id(0) * step_sources * 2
    products = []
    for item in range(2 * step_sources):
        ref = ref_ref[local_ref[first + item]]
        ref_real, ref_imag = ref[:, :side], ref[:, side:]
        filt_real, filt_imag = filt_ref[item, :, :side], filt_ref[item, :, side:]
        products.append(
            jnp.concatenate(
                [
                    filt_real * ref_real + filt_imag * ref_imag,
                    filt_imag * ref_real - filt_real * ref_imag,
                ],
                axis=1,
            )
        )
    high, low = split(jnp.concatenate(products, axis=0))
    by_col = jnp.dot(
        jnp.concatenate([high, low], axis=1), col_ref[...], preferred_element_type=jnp.float32
    )
    by_col = by_col[:, :side] + by_col[:, side:]
    lane = lax.broadcasted_iota(jnp.int32, (1, side), 1)
    for at in range(step_sources):
        sums = []
        for k in range(2):
            item = 2 * at + k
            total = jnp.sum(
                by_col[item * HALF : (item + 1) * HALF] * row_ref[...], axis=0, keepdims=True
            )
            sums.append(total + pltpu.roll(total, side // 2, axis=1))
        score_ref[at] = jnp.where(lane < side // 2, sums[0], sums[1])


def owner_spectra(images, contrast, turn, row, col, left, right, ready, class_local):
    sources, _, _, side = images.shape
    step_sources = 8
    whole = lambda x: pl.BlockSpec(x.shape, lambda i: (0,) * x.ndim)
    tables = (contrast, turn, row, col, left, right)
    half = jax.ShapeDtypeStruct((class_local // 2, HALF, 2 * side), jnp.float32)
    return pl.pallas_call(
        functools.partial(spectrum_kernel, step_sources),
        grid=(sources // step_sources,),
        out_shape=(
            half,
            half,
            jax.ShapeDtypeStruct((2 * sources, HALF, 2 * side), jnp.float32),
            jax.ShapeDtypeStruct((2 * sources,), jnp.int32),
        ),
        in_specs=[pl.BlockSpec(memory_space=pltpu.HBM)]
        + [whole(table) for table in tables]
        + [pl.BlockSpec(memory_space=pl.ANY)] * len(ready),
        out_specs=(
            pl.BlockSpec(memory_space=pltpu.HBM),
            pl.BlockSpec(memory_space=pltpu.HBM),
            pl.BlockSpec((2 * step_sources, HALF, 2 * side), lambda i: (i, 0, 0)),
            pl.BlockSpec(memory_space=pltpu.SMEM),
        ),
        scratch_shapes=[
            pltpu.VMEM((class_local, HALF, 2 * side), jnp.float32),
            pltpu.VMEM((sources, 2 * side, side), jnp.float32),
            pltpu.SMEM((sources, 1, side), jnp.float32),
            pltpu.SemaphoreType.DMA((2,)),
            pltpu.SemaphoreType.DMA((sources // step_sources,)),
            pltpu.SemaphoreType.DMA,
        ],
        compiler_params=pltpu.CompilerParams(vmem_limit_bytes=32 * MIB),
        name="owner_spectra",
    )(images, *tables, *ready)


def owner_scores(local, filtered, refs, col, row):
    items, _, wide = filtered.shape
    step_sources = 16
    whole = lambda x: pl.BlockSpec(x.shape, lambda i: (0,) * x.ndim)
    return pl.pallas_call(
        functools.partial(score_kernel, step_sources),
        grid=(items // 2 // step_sources,),
        out_shape=jax.ShapeDtypeStruct((items // 2, 1, wide // 2), jnp.float32),
        in_specs=[
            pl.BlockSpec(memory_space=pltpu.SMEM),
            pl.BlockSpec((2 * step_sources, HALF, wide), lambda i: (i, 0, 0)),
            whole(refs), whole(col), whole(row),
        ],
        out_specs=pl.BlockSpec((step_sources, 1, wide // 2), lambda i: (i, 0, 0)),
        compiler_params=pltpu.CompilerParams(vmem_limit_bytes=40 * MIB),
        name="owner_scores",
    )(local, filtered, refs, col, row)


def finish_kernel(target_ref, mine_ref, a_ref, b_ref, c_ref, contrast_ref, lanes_ref, unfold_ref, home_ref,
                  fresh_ref, score_ref):
    classes, _, _, side = fresh_ref.shape
    squares = [contrast_ref[which] * contrast_ref[which] for which in range(contrast_ref.shape[0])]
    ratios = []
    for at in range(classes):
        total = (mine_ref[at] + a_ref[at]) + (b_ref[at] + c_ref[at])
        weight = jnp.zeros((HALF, side), jnp.float32)
        for which, square in enumerate(squares):
            weight += total[COUNT : COUNT + 1, which : which + 1] * square
        inverse = 1.0 / (weight + 1.0)
        for part in range(2):
            ratio = total[:, part * side : (part + 1) * side] * inverse
            fresh_ref[at, part, : side // 2] = ratio[: side // 2]
            ratios.append(ratio)
    high, low = split(jnp.concatenate(ratios, axis=0))
    flipped = jnp.dot(high, lanes_ref[...], preferred_element_type=jnp.float32) + jnp.dot(
        low, lanes_ref[...], preferred_element_type=jnp.float32
    )
    flipped = [flipped[at * HALF : (at + 1) * HALF] for at in range(2 * classes)]
    pad = jnp.zeros((unfold_ref.shape[1] - HALF, 2 * classes * side), jnp.float32)
    high, low = split(jnp.concatenate([jnp.concatenate(flipped, axis=1), pad], axis=0))
    back = jnp.dot(unfold_ref[...], high, preferred_element_type=jnp.float32) + jnp.dot(
        unfold_ref[...], low, preferred_element_type=jnp.float32
    )
    for at in range(classes):
        for part in range(2):
            first = (2 * at + part) * side
            block = back[:, first : first + side]
            fresh_ref[at, part, side // 2 :] = block if part == 0 else -block
    items, shifts = score_ref.shape
    for item in range(items):
        target = target_ref[item]
        row = home_ref[lax.div(target, 2)]
        row = jnp.where(lax.rem(target, 2) == 1, pltpu.roll(row, shifts, axis=1), row)
        score_ref[item : item + 1, :] = row[:, :shifts]


def finish(target, blocks, contrast, lanes, unfold, home, side):
    return pl.pallas_call(
        finish_kernel,
        out_shape=(
            jax.ShapeDtypeStruct((blocks[0].shape[0], 2, side, side), jnp.float32),
            jax.ShapeDtypeStruct((target.shape[0], side // 2), jnp.float32),
        ),
        in_specs=[pl.BlockSpec(memory_space=pltpu.SMEM)] + [pl.BlockSpec(memory_space=pltpu.VMEM)] * 8,
        compiler_params=pltpu.CompilerParams(vmem_limit_bytes=16 * MIB),
        name="finish",
    )(target, *blocks, contrast, lanes, unfold, home)


def body(
    particles, references, class_of, rotation_bin, shift_best, defocus_bin, shift_list,
    defocus, chips_y,
):
    side = particles.shape[-1]
    class_local = references.shape[0]
    owners = lax.axis_size("cls")
    groups = lax.axis_size("grp")
    unit = 2.0 * math.pi / side

    cores = groups // chips_y
    own_classes = class_local // groups

    send = place_slots(
        particles, class_of, rotation_bin, shift_best, defocus_bin, shift_list, owners, class_local, chips_y
    )
    images = lax.all_to_all(send, "cls", split_axis=0, concat_axis=0, tiled=True)

    pixel = jnp.arange(side, dtype=jnp.int32)
    signed = jnp.where(pixel < side // 2, pixel, pixel - side).astype(jnp.float32)
    half = jnp.arange(HALF, dtype=jnp.int32)
    half_signed = jnp.where(half < side // 2, half, half - side).astype(jnp.float32)
    radius = (half_signed[:, None] ** 2 + signed[None, :] ** 2) / float((side // 2) ** 2)
    angle = defocus[:, None, None] * radius[None]
    contrast = -(0.995 * jnp.sin(angle) + 0.1 * jnp.cos(angle))

    row_angle = ((half[None, :] * shift_list[:, 0][:, None]) % side).astype(jnp.float32) * unit
    col_angle = ((pixel[None, :] * shift_list[:, 1][:, None]) % side).astype(jnp.float32) * unit
    row_cos, row_sin = jnp.cos(row_angle), jnp.sin(row_angle)
    col_cos, col_sin = jnp.cos(col_angle), jnp.sin(col_angle)
    col = jnp.concatenate(
        [
            jnp.concatenate([col_cos.T, col_sin.T], axis=1),
            jnp.concatenate([-col_sin.T, col_cos.T], axis=1),
        ],
        axis=0,
    )
    col_high = lax.reduce_precision(col, exponent_bits=8, mantissa_bits=7)
    col = jnp.concatenate([col_high, col - col_high], axis=1).astype(jnp.bfloat16)
    col = jnp.concatenate([col, col], axis=0)
    row = jnp.concatenate([row_cos.T, -row_sin.T], axis=1) / side

    lanes, fold, unfold = flip_constants(side)
    live_rows = (half <= side // 2).astype(jnp.float32)[:, None]
    folded = jnp.einsum("ua,ciab->ciub", fold, references, precision=lax.Precision.HIGH)
    folded = jnp.einsum("ciub,bv->ciuv", folded, lanes, precision=lax.Precision.HIGH)
    top = references[:, :, :HALF] * live_rows
    refs = jnp.concatenate([top[:, 0] + folded[:, 0], top[:, 1] - folded[:, 1]], axis=2)

    refs = pltpu.with_memory_space_constraint(refs, pltpu.HBM)
    left, right = dft_constants(side)
    best_row, best_col = shift_constants(side)
    keep, give, filtered, local = owner_spectra(
        images, contrast, jnp.asarray(turn_constants(side)), jnp.asarray(best_row),
        jnp.asarray(best_col), jnp.asarray(left), jnp.asarray(right), (refs, col, row), class_local,
    )
    slot_scores = owner_scores(local, filtered, refs, col, row)

    got = lax.ppermute(give, "grp", [(i, i ^ 1) for i in range(groups)])
    got, slot_scores = lax.optimization_barrier((got, slot_scores))
    blocks = {}
    for step in (2, 1, 3, 0):
        part = slice(step * own_classes, (step + 1) * own_classes)
        block = keep[part] + got[part]
        pairs = [(i, ((i // cores + step) % chips_y) * cores + i % cores) for i in range(groups)]
        blocks[step] = lax.ppermute(block, "grp", pairs) if step else block

    home = lax.all_to_all(slot_scores, "cls", split_axis=0, concat_axis=0, tiled=True)
    owner_of = class_of // class_local
    earlier = jnp.tril(owner_of[:, None] == owner_of[None, :], -1)
    target = owner_of * 2 + jnp.sum(earlier.astype(jnp.int32), axis=1)
    fresh_refs, scores = finish(
        target, [blocks[step] for step in range(chips_y)], contrast, jnp.asarray(lanes, jnp.bfloat16),
        jnp.asarray(unfold, jnp.bfloat16), home, side,
    )
    return (scores, fresh_refs)


def solution(mesh):
    chips_y = mesh.shape["grp"] // 2
    return jax.shard_map(
        functools.partial(body, chips_y=chips_y),
        mesh=mesh,
        in_specs=(
            P(("grp", "cls"), None, None),
            P("cls", None, None, None),
            P(("grp", "cls")),
            P(("grp", "cls")),
            P(("grp", "cls")),
            P(("grp", "cls")),
            P(),
            P(),
        ),
        out_specs=(P(("grp", "cls"), None), P(("cls", "grp"), None, None, None)),
        check_vma=False,
    )
```

```python
import functools
import math

import jax
import jax.numpy as jnp
import numpy as np
from jax import lax
from jax.experimental import pallas as pl
from jax.experimental.pallas import tpu as pltpu
from jax.sharding import PartitionSpec as P

HALF = 72
TAG = 8
COUNT = HALF - 1
SHIFT = 8
MIB = 1 << 20


def split_np(table):
    high = table.astype(jnp.bfloat16)
    low = (table - high.astype(np.float32)).astype(jnp.bfloat16)
    return high, low


def split(values):
    high = values.astype(jnp.bfloat16)
    low = (values - high.astype(jnp.float32)).astype(jnp.bfloat16)
    return high, low


def dft_constants(side):
    grid = np.outer(np.arange(side), np.arange(side)) % side
    angles = grid * (2.0 * np.pi / side)
    cos_table = (np.cos(angles) / np.sqrt(side)).astype(np.float32)
    sin_table = (np.sin(angles) / np.sqrt(side)).astype(np.float32)
    rows = side // 2 + 1
    left = np.zeros((2, HALF, side), np.float32)
    left[0, :rows] = cos_table[:rows]
    left[1, :rows] = sin_table[:rows]
    left_high, left_low = split_np(left.reshape(2 * HALF, side))
    left_table = np.concatenate(
        [
            np.concatenate([left_high, left_high], axis=1),
            np.concatenate([left_low, np.zeros_like(left_low)], axis=1),
        ],
        axis=0,
    )
    right = np.block([[cos_table, -sin_table], [-sin_table, -cos_table]]).astype(np.float32)
    right_high, right_low = split_np(right)
    return left_table, np.concatenate([right_high, right_high, right_low], axis=0)


def turn_constants(side):
    row = np.arange(HALF)[:, None] + 0 * np.arange(side)[None, :]
    col = 0 * np.arange(HALF)[:, None] + np.arange(side)[None, :]
    shifts = np.stack([0 * row, row, row + col, col]) % side
    angles = shifts * (2.0 * np.pi / side)
    return np.concatenate([np.cos(angles), np.sin(angles)], axis=2).astype(np.float32)


def shift_constants(side):
    steps = np.arange(-SHIFT, SHIFT + 1)[:, None]
    row = np.broadcast_to((steps * np.arange(HALF) % side)[:, :, None], (2 * SHIFT + 1, HALF, side))
    col = (steps * np.arange(side) % side)[:, None, :]
    return [
        np.concatenate([np.cos(t * (2.0 * np.pi / side)), np.sin(t * (2.0 * np.pi / side))], axis=2).astype(np.float32)
        for t in (row, col)
    ]


def flip_constants(side):
    lanes = np.zeros((side, side), np.float32)
    lanes[(-np.arange(side)) % side, np.arange(side)] = 1.0
    fold = np.zeros((HALF, side), np.float32)
    for u in range(1, side // 2):
        fold[u, side - u] = 1.0
    unfold = np.zeros((side // 2, HALF + 8), np.float32)
    for r in range(side // 2):
        unfold[r, side // 2 - r] = 1.0
    return lanes, fold, unfold


def scatter_kernel(class_local, chips_y, class_hbm, turn_hbm, best_hbm, bin_hbm, shift_hbm, image_ref, slot_ref,
                   class_ref, turn_ref, best_ref, bin_ref, shift_ref, count_ref, hold_ref, tag_ref,
                   int_sems, in_sems, out_sems, tag_sem):
    items, side, _ = hold_ref.shape
    pairs = ((class_hbm, class_ref), (turn_hbm, turn_ref), (best_hbm, best_ref), (bin_hbm, bin_ref), (shift_hbm, shift_ref))
    ints = [pltpu.make_async_copy(a, b, int_sems.at[at]) for at, (a, b) in enumerate(pairs)]
    for load in ints:
        load.start()
    loads = []
    for item in range(items):
        load = pltpu.make_async_copy(image_ref.at[item], hold_ref.at[item], in_sems.at[item])
        load.start()
        loads.append(load)
    for owner in range(count_ref.shape[0]):
        count_ref[owner] = 0
    tag_ref[...] = jnp.zeros_like(tag_ref)
    lane = lax.broadcasted_iota(jnp.int32, (1, side), 1)
    groups = lax.axis_size("grp")
    me_grp = lax.axis_index("grp")
    cores, own = groups // chips_y, class_local // groups
    core, me_y = lax.rem(me_grp, cores), lax.div(me_grp, cores)
    for load in ints:
        load.wait()
    stores = []
    for item in range(items):
        owner = lax.div(class_ref[item], class_local)
        rank = count_ref[owner]
        count_ref[owner] = rank + 1
        loads[item].wait()
        store = pltpu.make_async_copy(
            hold_ref.at[item],
            slot_ref.at[owner, pl.ds(pl.multiple_of(rank * side, side), side), 0, :],
            out_sems.at[item],
        )
        store.start()
        stores.append(store)
        local = class_ref[item] - owner * class_local
        place = lax.div(local, own)
        other = lax.rem(lax.rem(place, cores) - core + cores, cores)
        step = lax.rem(lax.div(place, cores) - me_y + chips_y, chips_y)
        target = (other * chips_y + step) * own + lax.rem(local, own)
        best = best_ref[item]
        fields = (local, turn_ref[item], shift_ref[0, best] + SHIFT, shift_ref[1, best] + SHIFT, bin_ref[item], target, 1)
        tag = jnp.zeros((1, side), jnp.int32)
        for at, value in enumerate(fields):
            tag = jnp.where(lane == rank * TAG + at, value, tag)
        tag_ref[owner] += tag.astype(jnp.float32)
    store = pltpu.make_async_copy(tag_ref, slot_ref.at[:, 2 * side], tag_sem)
    store.start()
    stores.append(store)
    for store in stores:
        store.wait()


def place_slots(particles, class_of, rotation_bin, shift_best, defocus_bin, shift_list, owners, class_local, chips_y):
    count, side, _ = particles.shape
    return pl.pallas_call(
        functools.partial(scatter_kernel, class_local, chips_y),
        out_shape=jax.ShapeDtypeStruct((owners, 2 * side + 1, 1, side), jnp.float32),
        in_specs=[pl.BlockSpec(memory_space=pltpu.HBM)] * 6,
        out_specs=pl.BlockSpec(memory_space=pltpu.HBM),
        scratch_shapes=[pltpu.SMEM((count,), jnp.int32)] * 4
        + [
            pltpu.SMEM(shift_list.shape[::-1], jnp.int32),
            pltpu.SMEM((owners,), jnp.int32),
            pltpu.VMEM((count, side, side), jnp.float32),
            pltpu.VMEM((owners, 1, side), jnp.float32),
            pltpu.SemaphoreType.DMA((5,)),
            pltpu.SemaphoreType.DMA((count,)),
            pltpu.SemaphoreType.DMA((count,)),
            pltpu.SemaphoreType.DMA,
        ],
        compiler_params=pltpu.CompilerParams(vmem_limit_bytes=58 * MIB),
        name="place_slots",
    )(class_of, rotation_bin, shift_best, defocus_bin, shift_list.T, particles)


def read_tag(tag_ref, source, slot, at):
    return tag_ref[source, 0, slot * TAG + at].astype(jnp.int32)


def spectrum_kernel(step_sources, image_ref, contrast_ref, turn_ref, row_ref, col_ref, left_ref, right_ref,
                    *refs):
    keep_ref, give_ref, filt_ref, local_ref, numer_ref, hold_ref, tag_ref, sems, in_sems, tag_sem = refs[-10:]
    side = image_ref.shape[-1]
    first = pl.program_id(0) * step_sources
    lane = lax.broadcasted_iota(jnp.int32, (1, side), 1)

    def load(step):
        part = pl.ds(step * step_sources, step_sources)
        return pltpu.make_async_copy(
            image_ref.at[part, pl.ds(0, 2 * side), 0, :], hold_ref.at[part], in_sems.at[step]
        )

    @pl.when(pl.program_id(0) == 0)
    def _():
        tags = pltpu.make_async_copy(image_ref.at[:, 2 * side], tag_ref, tag_sem)
        tags.start()
        load(0).start()
        numer_ref[...] = jnp.zeros_like(numer_ref)
        tags.wait()

    load(pl.program_id(0)).wait()

    @pl.when(pl.program_id(0) < pl.num_programs(0) - 1)
    def _():
        load(pl.program_id(0) + 1).start()

    turns = [read_tag(tag_ref, first + item // 2, item % 2, 1) for item in range(2 * step_sources)]
    parts = []
    for at in range(step_sources):
        highs, lows = [], []
        for k in range(2):
            image = hold_ref[first + at, k * side : (k + 1) * side]
            odd = lax.rem(turns[2 * at + k], 2) == 1
            high, low = split(jnp.where(odd, image.T, image))
            highs.append(high)
            lows.append(low)
        stacked = jnp.concatenate(
            [jnp.concatenate(highs, axis=1), jnp.concatenate(lows, axis=1)], axis=0
        )
        halfway = jnp.dot(left_ref[...], stacked, preferred_element_type=jnp.float32)
        halfway = halfway[: 2 * HALF] + halfway[2 * HALF :]
        for k in range(2):
            odd = lax.rem(turns[2 * at + k], 2) == 1
            sign = jnp.where(odd, -1.0, 1.0).astype(jnp.float32)
            lanes = slice(k * side, (k + 1) * side)
            parts.append(
                jnp.concatenate([halfway[:HALF, lanes], sign * halfway[HALF:, lanes]], axis=1)
            )
    high, low = split(jnp.concatenate(parts, axis=0))
    spectrum = jnp.dot(
        jnp.concatenate([high, low, high], axis=1), right_ref[...], preferred_element_type=jnp.float32
    )
    for item in range(2 * step_sources):
        info = [read_tag(tag_ref, first + item // 2, item % 2, at) for at in range(7)]
        local_ref[2 * first + item] = info[0]
        rows = slice(item * HALF, (item + 1) * HALF)
        sign = jnp.where(turns[item] >= 2, -1.0, 1.0).astype(jnp.float32)
        real = spectrum[rows, :side]
        imag = sign * spectrum[rows, side:]
        turn = turn_ref[turns[item]]
        contrast = contrast_ref[info[4]]
        turn_real, turn_imag = turn[:, :side], turn[:, side:]
        filt_real = contrast * (real * turn_real - imag * turn_imag)
        filt_imag = contrast * (real * turn_imag + imag * turn_real)
        filt_ref[item, :, :side] = filt_real
        filt_ref[item, :, side:] = filt_imag

        live = info[6] > 0
        target = info[5]
        row_real, row_imag = row_ref[info[2], :, :side], row_ref[info[2], :, side:]
        half_real = filt_real * row_real - filt_imag * row_imag
        half_imag = filt_real * row_imag + filt_imag * row_real
        col_real, col_imag = col_ref[info[3], :, :side], col_ref[info[3], :, side:]
        numer_ref[target, :, :side] += jnp.where(live, half_real * col_real - half_imag * col_imag, 0.0)
        numer_ref[target, :, side:] += jnp.where(live, half_real * col_imag + half_imag * col_real, 0.0)
        hit = ((lane == info[4]) & live).astype(jnp.float32)
        numer_ref[target, COUNT : COUNT + 1, :side] += hit

    @pl.when(pl.program_id(0) == pl.num_programs(0) - 1)
    def _():
        half = numer_ref.shape[0] // 2
        copies = [
            pltpu.make_async_copy(numer_ref.at[pl.ds(half, half)], give_ref, sems.at[0]),
            pltpu.make_async_copy(numer_ref.at[pl.ds(0, half)], keep_ref, sems.at[1]),
        ]
        for copy in copies:
            copy.start()
        for copy in copies:
            copy.wait()


def score_kernel(step_sources, local_ref, filt_ref, ref_ref, col_ref, row_ref, score_ref):
    side = score_ref.shape[-1]
    first = pl.program_id(0) * step_sources * 2
    products = []
    for item in range(2 * step_sources):
        ref = ref_ref[local_ref[first + item]]
        ref_real, ref_imag = ref[:, :side], ref[:, side:]
        filt_real, filt_imag = filt_ref[item, :, :side], filt_ref[item, :, side:]
        products.append(
            jnp.concatenate(
                [
                    filt_real * ref_real + filt_imag * ref_imag,
                    filt_imag * ref_real - filt_real * ref_imag,
                ],
                axis=1,
            )
        )
    high, low = split(jnp.concatenate(products, axis=0))
    by_col = jnp.dot(
        jnp.concatenate([high, low], axis=1), col_ref[...], preferred_element_type=jnp.float32
    )
    by_col = by_col[:, :side] + by_col[:, side:]
    lane = lax.broadcasted_iota(jnp.int32, (1, side), 1)
    for at in range(step_sources):
        sums = []
        for k in range(2):
            item = 2 * at + k
            total = jnp.sum(
                by_col[item * HALF : (item + 1) * HALF] * row_ref[...], axis=0, keepdims=True
            )
            sums.append(total + pltpu.roll(total, side // 2, axis=1))
        score_ref[at] = jnp.where(lane < side // 2, sums[0], sums[1])


def owner_spectra(images, contrast, turn, row, col, left, right, ready, class_local):
    sources, _, _, side = images.shape
    step_sources = 8
    whole = lambda x: pl.BlockSpec(x.shape, lambda i: (0,) * x.ndim)
    tables = (contrast, turn, row, col, left, right)
    half = jax.ShapeDtypeStruct((class_local // 2, HALF, 2 * side), jnp.float32)
    return pl.pallas_call(
        functools.partial(spectrum_kernel, step_sources),
        grid=(sources // step_sources,),
        out_shape=(
            half,
            half,
            jax.ShapeDtypeStruct((2 * sources, HALF, 2 * side), jnp.float32),
            jax.ShapeDtypeStruct((2 * sources,), jnp.int32),
        ),
        in_specs=[pl.BlockSpec(memory_space=pltpu.HBM)]
        + [whole(table) for table in tables]
        + [pl.BlockSpec(memory_space=pl.ANY)] * len(ready),
        out_specs=(
            pl.BlockSpec(memory_space=pltpu.HBM),
            pl.BlockSpec(memory_space=pltpu.HBM),
            pl.BlockSpec((2 * step_sources, HALF, 2 * side), lambda i: (i, 0, 0)),
            pl.BlockSpec(memory_space=pltpu.SMEM),
        ),
        scratch_shapes=[
            pltpu.VMEM((class_local, HALF, 2 * side), jnp.float32),
            pltpu.VMEM((sources, 2 * side, side), jnp.float32),
            pltpu.SMEM((sources, 1, side), jnp.float32),
            pltpu.SemaphoreType.DMA((2,)),
            pltpu.SemaphoreType.DMA((sources // step_sources,)),
            pltpu.SemaphoreType.DMA,
        ],
        compiler_params=pltpu.CompilerParams(vmem_limit_bytes=32 * MIB),
        name="owner_spectra",
    )(images, *tables, *ready)


def owner_scores(local, filtered, refs, col, row):
    items, _, wide = filtered.shape
    step_sources = 32
    whole = lambda x: pl.BlockSpec(x.shape, lambda i: (0,) * x.ndim)
    return pl.pallas_call(
        functools.partial(score_kernel, step_sources),
        grid=(items // 2 // step_sources,),
        out_shape=jax.ShapeDtypeStruct((items // 2, 1, wide // 2), jnp.float32),
        in_specs=[
            pl.BlockSpec(memory_space=pltpu.SMEM),
            pl.BlockSpec((2 * step_sources, HALF, wide), lambda i: (i, 0, 0)),
            whole(refs), whole(col), whole(row),
        ],
        out_specs=pl.BlockSpec((step_sources, 1, wide // 2), lambda i: (i, 0, 0)),
        compiler_params=pltpu.CompilerParams(vmem_limit_bytes=40 * MIB),
        name="owner_scores",
    )(local, filtered, refs, col, row)


def finish_kernel(target_ref, mine_ref, a_ref, b_ref, c_ref, contrast_ref, lanes_ref, unfold_ref, home_ref,
                  fresh_ref, score_ref):
    classes, _, _, side = fresh_ref.shape
    squares = [contrast_ref[which] * contrast_ref[which] for which in range(contrast_ref.shape[0])]
    ratios = []
    for at in range(classes):
        total = (mine_ref[at] + a_ref[at]) + (b_ref[at] + c_ref[at])
        weight = jnp.zeros((HALF, side), jnp.float32)
        for which, square in enumerate(squares):
            weight += total[COUNT : COUNT + 1, which : which + 1] * square
        inverse = 1.0 / (weight + 1.0)
        for part in range(2):
            ratio = total[:, part * side : (part + 1) * side] * inverse
            fresh_ref[at, part, : side // 2] = ratio[: side // 2]
            ratios.append(ratio)
    high, low = split(jnp.concatenate(ratios, axis=0))
    flipped = jnp.dot(high, lanes_ref[...], preferred_element_type=jnp.float32) + jnp.dot(
        low, lanes_ref[...], preferred_element_type=jnp.float32
    )
    flipped = [flipped[at * HALF : (at + 1) * HALF] for at in range(2 * classes)]
    pad = jnp.zeros((unfold_ref.shape[1] - HALF, 2 * classes * side), jnp.float32)
    high, low = split(jnp.concatenate([jnp.concatenate(flipped, axis=1), pad], axis=0))
    back = jnp.dot(unfold_ref[...], high, preferred_element_type=jnp.float32) + jnp.dot(
        unfold_ref[...], low, preferred_element_type=jnp.float32
    )
    for at in range(classes):
        for part in range(2):
            first = (2 * at + part) * side
            block = back[:, first : first + side]
            fresh_ref[at, part, side // 2 :] = block if part == 0 else -block
    items, shifts = score_ref.shape
    for item in range(items):
        target = target_ref[item]
        row = home_ref[lax.div(target, 2)]
        row = jnp.where(lax.rem(target, 2) == 1, pltpu.roll(row, shifts, axis=1), row)
        score_ref[item : item + 1, :] = row[:, :shifts]


def finish(target, blocks, contrast, lanes, unfold, home, side):
    return pl.pallas_call(
        finish_kernel,
        out_shape=(
            jax.ShapeDtypeStruct((blocks[0].shape[0], 2, side, side), jnp.float32),
            jax.ShapeDtypeStruct((target.shape[0], side // 2), jnp.float32),
        ),
        in_specs=[pl.BlockSpec(memory_space=pltpu.SMEM)] + [pl.BlockSpec(memory_space=pltpu.VMEM)] * 8,
        compiler_params=pltpu.CompilerParams(vmem_limit_bytes=16 * MIB),
        name="finish",
    )(target, *blocks, contrast, lanes, unfold, home)


def body(
    particles, references, class_of, rotation_bin, shift_best, defocus_bin, shift_list,
    defocus, chips_y,
):
    side = particles.shape[-1]
    class_local = references.shape[0]
    owners = lax.axis_size("cls")
    groups = lax.axis_size("grp")
    unit = 2.0 * math.pi / side

    cores = groups // chips_y
    own_classes = class_local // groups

    send = place_slots(
        particles, class_of, rotation_bin, shift_best, defocus_bin, shift_list, owners, class_local, chips_y
    )
    images = lax.all_to_all(send, "cls", split_axis=0, concat_axis=0, tiled=True)

    pixel = jnp.arange(side, dtype=jnp.int32)
    signed = jnp.where(pixel < side // 2, pixel, pixel - side).astype(jnp.float32)
    half = jnp.arange(HALF, dtype=jnp.int32)
    half_signed = jnp.where(half < side // 2, half, half - side).astype(jnp.float32)
    radius = (half_signed[:, None] ** 2 + signed[None, :] ** 2) / float((side // 2) ** 2)
    angle = defocus[:, None, None] * radius[None]
    contrast = -(0.995 * jnp.sin(angle) + 0.1 * jnp.cos(angle))

    row_angle = ((half[None, :] * shift_list[:, 0][:, None]) % side).astype(jnp.float32) * unit
    col_angle = ((pixel[None, :] * shift_list[:, 1][:, None]) % side).astype(jnp.float32) * unit
    row_cos, row_sin = jnp.cos(row_angle), jnp.sin(row_angle)
    col_cos, col_sin = jnp.cos(col_angle), jnp.sin(col_angle)
    col = jnp.concatenate(
        [
            jnp.concatenate([col_cos.T, col_sin.T], axis=1),
            jnp.concatenate([-col_sin.T, col_cos.T], axis=1),
        ],
        axis=0,
    )
    col_high = lax.reduce_precision(col, exponent_bits=8, mantissa_bits=7)
    col = jnp.concatenate([col_high, col - col_high], axis=1).astype(jnp.bfloat16)
    col = jnp.concatenate([col, col], axis=0)
    row = jnp.concatenate([row_cos.T, -row_sin.T], axis=1) / side

    lanes, fold, unfold = flip_constants(side)
    live_rows = (half <= side // 2).astype(jnp.float32)[:, None]
    folded = jnp.einsum("ua,ciab->ciub", fold, references, precision=lax.Precision.HIGH)
    folded = jnp.einsum("ciub,bv->ciuv", folded, lanes, precision=lax.Precision.HIGH)
    top = references[:, :, :HALF] * live_rows
    refs = jnp.concatenate([top[:, 0] + folded[:, 0], top[:, 1] - folded[:, 1]], axis=2)

    refs = pltpu.with_memory_space_constraint(refs, pltpu.HBM)
    left, right = dft_constants(side)
    best_row, best_col = shift_constants(side)
    keep, give, filtered, local = owner_spectra(
        images, contrast, jnp.asarray(turn_constants(side)), jnp.asarray(best_row),
        jnp.asarray(best_col), jnp.asarray(left), jnp.asarray(right), (refs, col, row), class_local,
    )
    slot_scores = owner_scores(local, filtered, refs, col, row)

    got = lax.ppermute(give, "grp", [(i, i ^ 1) for i in range(groups)])
    got, slot_scores = lax.optimization_barrier((got, slot_scores))
    blocks = {}
    for step in (2, 1, 3, 0):
        part = slice(step * own_classes, (step + 1) * own_classes)
        block = keep[part] + got[part]
        pairs = [(i, ((i // cores + step) % chips_y) * cores + i % cores) for i in range(groups)]
        blocks[step] = lax.ppermute(block, "grp", pairs) if step else block

    home = lax.all_to_all(slot_scores, "cls", split_axis=0, concat_axis=0, tiled=True)
    owner_of = class_of // class_local
    earlier = jnp.tril(owner_of[:, None] == owner_of[None, :], -1)
    target = owner_of * 2 + jnp.sum(earlier.astype(jnp.int32), axis=1)
    fresh_refs, scores = finish(
        target, [blocks[step] for step in range(chips_y)], contrast, jnp.asarray(lanes, jnp.bfloat16),
        jnp.asarray(unfold, jnp.bfloat16), home, side,
    )
    return (scores, fresh_refs)


def solution(mesh):
    chips_y = mesh.shape["grp"] // 2
    return jax.shard_map(
        functools.partial(body, chips_y=chips_y),
        mesh=mesh,
        in_specs=(
            P(("grp", "cls"), None, None),
            P("cls", None, None, None),
            P(("grp", "cls")),
            P(("grp", "cls")),
            P(("grp", "cls")),
            P(("grp", "cls")),
            P(),
            P(),
        ),
        out_specs=(P(("grp", "cls"), None), P(("cls", "grp"), None, None, None)),
        check_vma=False,
    )
```
